128 devices in a mesh: vv: 64 (over z, y, x_hi, core), grp: 2 (over x_lo).
Axes of the slice: x: 4 (x_hi: 2, x_lo: 2; x = x_hi * 2 + x_lo), y: 4, z: 4, core: 2. Of those that a mesh axis runs over, the one named last changes fastest.
Arguments:
- integrals: bfloat16 [64, 4608, 1536], P('vv', 'grp'), may hold values from -0.15625 to 0.15625
- amplitudes: bfloat16 [2048, 12288], P('grp'), may hold values from -6 to 6
- orbital_irrep: int32 [768], replicated, may hold values from 0 to 7, as said below
- pair_irrep: int32 [64], P('vv'), may hold values from 0 to 7, as said below
- panel_block: int32 [1], replicated, may hold values from 0 to 7
Outputs:
- residual: bfloat16 [2048, 64, 4608], P('vv', None, 'grp')
The draws below stay inside these ranges and needn't reach their ends.
Inputs may be any that keep to these rules, and one draw needn't show every extreme that they name: `orbital_irrep`: constant over each aligned run of 96 orbitals; the 8 runs carry different irreps. `pair_irrep`: every irrep is owned by some index.
All inputs are finite; a program needn't handle non-finite values.
Results may differ from the reference program's by a relative error of at most 0.001.
Values may be sent and summed in bfloat16 or wider, within the bound.
A program may use at most 256 MiB of HBM per device.

```python
import jax
import jax.numpy as jnp
from jax import lax

NIRR = 8
BS = 96
NV = 768
DW = 16
KP = 1536
ROWS_GRP = 4608
IJ = 2048
N_VV = 64


def draw_orbital_irrep(key, part):
    key = jax.random.fold_in(key, 11)
    labels = jax.random.permutation(key, NIRR)
    return jnp.repeat(labels, BS).astype(jnp.int32)


def draw_pair_irrep(key, part):
    key = jax.random.fold_in(key, 23)
    order = jax.random.permutation(key, N_VV)
    return (order % NIRR).astype(jnp.int32)


def block_levels(stream_key, shape, shards, low, top_value):
    level, own = 1.0, jax.random.fold_in(stream_key, 6)
    for dim, blocks in shards:
        draws = jnp.exp(jax.random.uniform(jax.random.fold_in(own, dim), (blocks,), jnp.float32, low / len(shards), top_value / len(shards)))
        level = level * jnp.repeat(draws, shape[dim] // blocks).reshape([-1 if axis == dim else 1 for axis in range(len(shape))])
    return level


def gaussian(stream_key, dims, scale, limit, shards=(), held_as=jnp.bfloat16):
    drawn = scale * jax.random.normal(stream_key, dims, jnp.float32)
    if shards:
        drawn = drawn * block_levels(stream_key, dims, shards, -0.22, 0.18)
    return jnp.clip(drawn, -limit, limit).astype(held_as)


def setup_inputs(seed: int = 0) -> dict:
    keys = jax.random.split(jax.random.key(seed), 6)
    integrals = gaussian(keys[0], (N_VV, ROWS_GRP, KP), KP ** -0.5, 0.15625, ((0, 64), (1, 2)))
    amplitudes = gaussian(keys[1], (IJ, DW * NV), 1.0, 6.0, ((0, 2),))
    orbital_irrep = draw_orbital_irrep(jax.random.fold_in(keys[5], 71), 0)
    pair_irrep = draw_pair_irrep(jax.random.fold_in(keys[5], 71), 0)
    panel_block = jax.random.randint(keys[4], (1,), 0, NIRR).astype(jnp.int32)
    return {"integrals": integrals, "amplitudes": amplitudes, "orbital_irrep": orbital_irrep, "pair_irrep": pair_irrep, "panel_block": panel_block}


def reference(integrals, amplitudes, orbital_irrep, pair_irrep, panel_block):
    block_irrep = orbital_irrep.reshape(NIRR, BS)[:, 0]
    block_index = jnp.arange(NIRR, dtype=jnp.int32)
    panel_irrep = jnp.sum(jnp.where(block_index == panel_block[0], block_irrep, 0)).astype(jnp.int32)
    shaped = amplitudes.reshape(IJ, DW, NIRR, BS)

    def one_owner(inputs):
        integral_rows, owner_irrep = inputs
        target = jnp.bitwise_xor(owner_irrep, panel_irrep)
        allowed = jnp.sum(jnp.where(block_irrep == target, block_index, 0)).astype(jnp.int32)
        chosen = lax.dynamic_slice_in_dim(shaped, allowed, 1, 2).reshape(IJ, DW * BS)
        return jnp.dot(chosen, integral_rows.T, preferred_element_type=jnp.float32)

    stacked = lax.map(one_owner, (integrals, pair_irrep))
    return jnp.transpose(stacked, (1, 0, 2)).astype(jnp.bfloat16)
```

```python
import functools

import jax
import jax.numpy as jnp
from jax import lax
from jax.experimental import pallas as pl
from jax.experimental.pallas import tpu as pltpu
from jax.sharding import PartitionSpec as P

NIRR = 8
BS = 96
DW = 16
NV = NIRR * BS
KP = DW * BS
ROWS = 2304
IJ = 2048
HALF = IJ // 2
N_VV = 64
OWN = IJ // N_VV
BLOCK = 256
PER_BLOCK = BLOCK // OWN
CHUNK = 128
NCOL = 768
MESH = pl.DeviceIdType.MESH
SLICE_ROWS = 256
MIB = 1024 * 1024


def slice_kernel(row0, nblocks, orb, pair, panel, amp, out, win, outbuf, in_sem, out_sem):
    target = pair[0] ^ orb[panel[0] * BS]
    allowed = jnp.int32(0)
    for k in range(NIRR):
        allowed += jnp.where(orb[k * BS] == target, jnp.int32(k), jnp.int32(0))
    tile = jnp.minimum(allowed * BS // 128, 4)
    off = allowed * BS - tile * 128

    def window(b, d):
        return pltpu.make_async_copy(
            amp.at[pl.ds(row0 + b * SLICE_ROWS, SLICE_ROWS), pl.ds(pl.multiple_of(d * NV + tile * 128, 128), 256)],
            win.at[b, d],
            in_sem.at[b],
        )

    def result(b):
        return pltpu.make_async_copy(outbuf.at[b], out.at[pl.ds(b * SLICE_ROWS, SLICE_ROWS)], out_sem.at[b])

    for b in range(nblocks):
        for d in range(DW):
            window(b, d).start()
    lane = lax.broadcasted_iota(jnp.int32, (SLICE_ROWS, 128), 1)

    for b in range(nblocks):
        for d in range(DW):
            window(b, d).wait()

        @pl.loop(0, DW // 4)
        def _(q):
            w = [
                pltpu.roll(win[b, q * 4 + j].astype(jnp.float32), lax.rem((96 * j) % 128 - off + 512, 256), 1)
                for j in range(4)
            ]
            t0 = jnp.where(lane < 96, w[0][:, :128], w[1][:, :128])
            t1 = jnp.where(lane < 64, w[1][:, 128:], w[2][:, :128])
            t2 = jnp.where(lane < 32, w[2][:, 128:], w[3][:, :128])
            base = pl.multiple_of(q * 384, 128)
            outbuf[b, :, pl.ds(base, 384)] = jnp.concatenate([t0, t1, t2], axis=1).astype(jnp.bfloat16)

        result(b).start()
    for b in range(nblocks):
        result(b).wait()


def slice_block(row0, rows, orb, pair, panel, amp):
    nblocks = rows // SLICE_ROWS
    smem = pl.BlockSpec(memory_space=pltpu.SMEM)
    hbm = pl.BlockSpec(memory_space=pl.ANY)
    return pl.pallas_call(
        functools.partial(slice_kernel, row0, nblocks),
        name="slice_block",
        out_shape=jax.ShapeDtypeStruct((rows, KP), jnp.bfloat16),
        in_specs=[smem, smem, smem, hbm],
        out_specs=hbm,
        scratch_shapes=[
            pltpu.VMEM((nblocks, DW, SLICE_ROWS, 256), jnp.bfloat16),
            pltpu.VMEM((nblocks, SLICE_ROWS, KP), jnp.bfloat16),
            pltpu.SemaphoreType.DMA((nblocks,)),
            pltpu.SemaphoreType.DMA((nblocks,)),
        ],
        compiler_params=pltpu.CompilerParams(vmem_limit_bytes=40 * MIB),
        cost_estimate=pl.CostEstimate(flops=0, bytes_accessed=rows * 11264, transcendentals=0),
    )(orb, pair, panel, amp)


def ladder_kernel(own, other, integrals, recv, a, b, prod, load_sem, give_sem, get_sem, send_sem, recv_sem, self_sem):
    v = lax.axis_index("vv")
    g = lax.axis_index("grp")
    h = 1 - g
    flip = v + 2 - 4 * lax.rem(v // 2, 2)
    load_b = pltpu.make_async_copy(integrals.at[0], b, load_sem.at[0])
    load_a = pltpu.make_async_copy(own, a.at[pl.ds(g * HALF, HALF)], load_sem.at[1])
    load_a.start()
    load_b.start()

    barrier = pltpu.get_barrier_semaphore()

    @pl.loop(1, N_VV)
    def _(k):
        pl.semaphore_signal(barrier, inc=1, device_id=(lax.rem(v + k, N_VV), g), device_id_type=MESH)

    pl.semaphore_signal(barrier, inc=1, device_id=(v, h), device_id_type=MESH)
    pl.semaphore_signal(barrier, inc=1, device_id=(flip, h), device_id_type=MESH)
    pl.semaphore_wait(barrier, N_VV + 1)

    n_chunks = HALF // 2 // CHUNK

    def gives(j):
        first = pltpu.make_async_remote_copy(
            src_ref=own.at[pl.ds(j * CHUNK, CHUNK)],
            dst_ref=a.at[pl.ds(g * HALF + j * CHUNK, CHUNK)],
            send_sem=give_sem,
            recv_sem=get_sem.at[j],
            device_id=(v, h),
            device_id_type=MESH,
        )
        second = pltpu.make_async_remote_copy(
            src_ref=other.at[pl.ds(j * CHUNK, CHUNK)],
            dst_ref=a.at[pl.ds(g * HALF + HALF // 2 + j * CHUNK, CHUNK)],
            send_sem=give_sem,
            recv_sem=get_sem.at[n_chunks + j],
            device_id=(flip, h),
            device_id_type=MESH,
        )
        return first, second

    for j in range(n_chunks):
        for c in gives(j):
            c.start()
    load_a.wait()
    load_b.wait()

    rot = lax.rem(v // 8, 4)

    @pl.loop(0, IJ // BLOCK)
    def _(i):
        part = i // 4
        half = lax.rem(g + part, 2)
        q = lax.rem(i + rot, 4)

        @pl.when(part == 1)
        def _():
            for s in range(BLOCK // CHUNK):
                idx = q * (BLOCK // CHUNK) + s
                here = a.at[pl.ds(h * HALF + idx * CHUNK, CHUNK)]
                pltpu.make_async_remote_copy(here, here, give_sem, get_sem.at[idx], device_id=(v, h), device_id_type=MESH).wait_recv()

        row = pl.multiple_of(half * HALF + q * BLOCK, BLOCK)
        w0 = half * (N_VV // 2) + q * PER_BLOCK

        @pl.loop(0, ROWS // NCOL)
        def _(n):
            col = pl.multiple_of(n * NCOL, NCOL)
            y = lax.dot_general(
                a[pl.ds(row, BLOCK), :],
                b[pl.ds(col, NCOL), :],
                (((1,), (1,)), ((), ())),
                preferred_element_type=jnp.float32,
            )
            prod[pl.ds(w0, PER_BLOCK), :, pl.ds(col, NCOL)] = y.astype(jnp.bfloat16).reshape(PER_BLOCK, OWN, NCOL)

        @pl.loop(0, PER_BLOCK)
        def _(t):
            w = w0 + lax.rem(t + v, PER_BLOCK)

            @pl.when(w == v)
            def _():
                pltpu.make_async_copy(prod.at[v], recv.at[v], self_sem).start()

            @pl.when(w != v)
            def _():
                pltpu.make_async_remote_copy(
                    src_ref=prod.at[w],
                    dst_ref=recv.at[v],
                    send_sem=send_sem,
                    recv_sem=recv_sem,
                    device_id=(w, g),
                    device_id_type=MESH,
                ).start()

    for j in range(n_chunks):
        for c in gives(j):
            c.wait_send()
    pltpu.make_async_copy(prod.at[v], recv.at[v], self_sem).wait()
    rest = pltpu.make_async_remote_copy(
        src_ref=prod.at[pl.ds(0, N_VV - 1)],
        dst_ref=recv.at[pl.ds(0, N_VV - 1)],
        send_sem=send_sem,
        recv_sem=recv_sem,
        device_id=(v, h),
        device_id_type=MESH,
    )
    rest.wait_send()
    rest.wait_recv()


def ladder(own, other, integrals):
    hbm = pl.BlockSpec(memory_space=pl.ANY)
    return pl.pallas_call(
        ladder_kernel,
        name="ladder",
        out_shape=jax.ShapeDtypeStruct((N_VV, OWN, ROWS), jnp.bfloat16),
        in_specs=[hbm] * 3,
        out_specs=hbm,
        scratch_shapes=[
            pltpu.VMEM((IJ, KP), jnp.bfloat16),
            pltpu.VMEM((ROWS, KP), jnp.bfloat16),
            pltpu.VMEM((N_VV, OWN, ROWS), jnp.bfloat16),
            pltpu.SemaphoreType.DMA((2,)),
            pltpu.SemaphoreType.DMA,
            pltpu.SemaphoreType.DMA((HALF // CHUNK,)),
            pltpu.SemaphoreType.DMA,
            pltpu.SemaphoreType.DMA,
            pltpu.SemaphoreType.DMA,
        ],
        compiler_params=pltpu.CompilerParams(
            collective_id=0, has_side_effects=True, vmem_limit_bytes=48 * MIB
        ),
        cost_estimate=pl.CostEstimate(flops=2 * IJ * ROWS * KP, bytes_accessed=40 * MIB, transcendentals=0),
    )(own, other, integrals)


TCOL = 256


def swap_kernel(x, out):
    row = lax.broadcasted_iota(jnp.int32, (256, 256), 0)
    col = lax.broadcasted_iota(jnp.int32, (256, 256), 1)
    perm = jnp.where(lax.rem(row, 16) * 16 + row // 16 == col, 1.0, 0.0).astype(jnp.bfloat16)
    for i in range(OWN // 16):
        for s in range(N_VV // 16):
            block = x[pl.ds(s * 16, 16), pl.ds(i * 16, 16), :].reshape(256, TCOL)
            y = jnp.dot(perm, block, preferred_element_type=jnp.float32)
            out[pl.ds(i * 16, 16), pl.ds(s * 16, 16), :] = y.astype(jnp.bfloat16).reshape(16, 16, TCOL)


def swap(x):
    return pl.pallas_call(
        swap_kernel,
        name="swap",
        grid=(ROWS // TCOL,),
        out_shape=jax.ShapeDtypeStruct((OWN, N_VV, ROWS), jnp.bfloat16),
        in_specs=[pl.BlockSpec((N_VV, OWN, TCOL), lambda i: (0, 0, i))],
        out_specs=pl.BlockSpec((OWN, N_VV, TCOL), lambda i: (0, 0, i)),
        compiler_params=pltpu.CompilerParams(vmem_limit_bytes=32 * MIB),
        cost_estimate=pl.CostEstimate(flops=0, bytes_accessed=2 * IJ * ROWS * 2, transcendentals=0),
    )(x)


def shards(integrals, amplitudes, orbital_irrep, pair_irrep, panel_block):
    flipped = [(i, i ^ 2) for i in range(N_VV)]
    other_irrep = lax.ppermute(pair_irrep, "vv", flipped)
    own = slice_block(0, HALF, orbital_irrep, pair_irrep, panel_block, amplitudes)
    other = slice_block(HALF // 2, HALF // 2, orbital_irrep, other_irrep, panel_block, amplitudes)
    return swap(ladder(own, other, integrals))


def solution(mesh):
    return jax.shard_map(
        shards,
        mesh=mesh,
        in_specs=(P("vv", "grp", None), P("grp", None), P(), P("vv"), P()),
        out_specs=P("vv", None, "grp"),
        check_vma=False,
    )
```

```python
import functools

import jax
import jax.numpy as jnp
from jax import lax
from jax.experimental import pallas as pl
from jax.experimental.pallas import tpu as pltpu
from jax.sharding import PartitionSpec as P

NIRR = 8
BS = 96
DW = 16
NV = NIRR * BS
KP = DW * BS
ROWS = 2304
IJ = 2048
HALF = IJ // 2
N_VV = 64
OWN = IJ // N_VV
CHUNK = 128
WINDOW = 3
MESH = pl.DeviceIdType.MESH
SLICE_ROWS = 512
SUB_ROWS = 128
MIB = 1024 * 1024


def slice_kernel(row0, nblocks, orb, pair, panel, amp, out, win, outbuf, in_sem, out_sem):
    target = pair[0] ^ orb[panel[0] * BS]
    allowed = jnp.int32(0)
    for k in range(NIRR):
        allowed += jnp.where(orb[k * BS] == target, jnp.int32(k), jnp.int32(0))
    tile = jnp.minimum(allowed * BS // 128, 4)
    off = allowed * BS - tile * 128
    units = [(b, q) for b in range(nblocks) for q in range(DW // 4)]

    def window(b, q, j):
        d = q * 4 + j
        return pltpu.make_async_copy(
            amp.at[pl.ds(row0 + b * SLICE_ROWS, SLICE_ROWS), pl.ds(pl.multiple_of(d * NV + tile * 128, 128), 256)],
            win.at[d, pl.ds(b * SLICE_ROWS, SLICE_ROWS)],
            in_sem.at[b, q],
        )

    def result(b, q):
        part = (pl.ds(b * SLICE_ROWS, SLICE_ROWS), pl.ds(q * 4 * BS, 4 * BS))
        return pltpu.make_async_copy(outbuf.at[part], out.at[part], out_sem.at[b, q])

    for b, q in units:
        for j in range(4):
            window(b, q, j).start()
    lane = lax.broadcasted_iota(jnp.int32, (SUB_ROWS, 128), 1)

    for b, q in units:
        for j in range(4):
            window(b, q, j).wait()

        @pl.loop(0, SLICE_ROWS // SUB_ROWS)
        def _(r):
            rows = pl.ds(pl.multiple_of(b * SLICE_ROWS + r * SUB_ROWS, SUB_ROWS), SUB_ROWS)
            w = [
                pltpu.roll(win[q * 4 + j, rows].astype(jnp.float32), lax.rem((96 * j) % 128 - off + 512, 256), 1)
                for j in range(4)
            ]
            t0 = jnp.where(lane < 96, w[0][:, :128], w[1][:, :128])
            t1 = jnp.where(lane < 64, w[1][:, 128:], w[2][:, :128])
            t2 = jnp.where(lane < 32, w[2][:, 128:], w[3][:, :128])
            outbuf[rows, q * 384 : (q + 1) * 384] = jnp.concatenate([t0, t1, t2], axis=1).astype(jnp.bfloat16)

        result(b, q).start()
    for b, q in units:
        result(b, q).wait()


def slice_block(row0, rows, orb, pair, panel, amp):
    nblocks = rows // SLICE_ROWS
    smem = pl.BlockSpec(memory_space=pltpu.SMEM)
    hbm = pl.BlockSpec(memory_space=pl.ANY)
    return pl.pallas_call(
        functools.partial(slice_kernel, row0, nblocks),
        name="slice_block",
        out_shape=jax.ShapeDtypeStruct((rows, KP), jnp.bfloat16),
        in_specs=[smem, smem, smem, hbm],
        out_specs=hbm,
        scratch_shapes=[
            pltpu.VMEM((DW, rows, 256), jnp.bfloat16),
            pltpu.VMEM((rows, KP), jnp.bfloat16),
            pltpu.SemaphoreType.DMA((nblocks, DW // 4)),
            pltpu.SemaphoreType.DMA((nblocks, DW // 4)),
        ],
        compiler_params=pltpu.CompilerParams(vmem_limit_bytes=44 * MIB),
        cost_estimate=pl.CostEstimate(flops=0, bytes_accessed=rows * 11264, transcendentals=0),
    )(orb, pair, panel, amp)


def ladder_kernel(own, other, integrals, recv, a, b, prod, stage, load_sem, give_sem, get_sem, send_sem, recv_sem, self_sem, x_send, x_recv):
    v = lax.axis_index("vv")
    g = lax.axis_index("grp")
    h = 1 - g
    z, y = v // 16, lax.rem(v // 4, 4)
    xh, c = lax.rem(v // 2, 2), lax.rem(v, 2)
    flip = v + 2 - 4 * xh
    turn = 1 - 2 * c
    load_b = pltpu.make_async_copy(integrals.at[0], b, load_sem.at[0])
    load_a = pltpu.make_async_copy(own, a.at[pl.ds(g * HALF, HALF)], load_sem.at[1])
    load_a.start()
    load_b.start()

    barrier = pltpu.get_barrier_semaphore()

    def greet(w, group):
        pl.semaphore_signal(barrier, inc=1, device_id=(w, group), device_id_type=MESH)

    greet(flip, g)
    greet(v, h)
    greet(flip, h)

    @pl.loop(1, N_VV // 2)
    def _(k):
        p = lax.rem(v // 4 * 2 + c + k, N_VV // 2)
        greet(p // 2 * 4 + xh * 2 + lax.rem(p, 2), g)

    pl.semaphore_wait(barrier, N_VV // 2 + 2)

    n_chunks = HALF // 2 // CHUNK

    def gives(j):
        first = pltpu.make_async_remote_copy(
            src_ref=own.at[pl.ds(j * CHUNK, CHUNK)],
            dst_ref=a.at[pl.ds(g * HALF + j * CHUNK, CHUNK)],
            send_sem=give_sem,
            recv_sem=get_sem.at[j],
            device_id=(v, h),
            device_id_type=MESH,
        )
        second = pltpu.make_async_remote_copy(
            src_ref=other.at[pl.ds(j * CHUNK, CHUNK)],
            dst_ref=a.at[pl.ds(g * HALF + HALF // 2 + j * CHUNK, CHUNK)],
            send_sem=give_sem,
            recv_sem=get_sem.at[n_chunks + j],
            device_id=(flip, h),
            device_id_type=MESH,
        )
        return first, second

    for j in range(n_chunks):
        for copy in gives(lax.rem(y + turn * j + 4, 4)):
            copy.start()
    load_a.wait()
    load_b.wait()

    def multiply(row, w0, rows, cols):
        @pl.loop(0, ROWS // cols)
        def _(n):
            col = pl.multiple_of(n * cols, cols)
            part = lax.dot_general(
                a[pl.ds(pl.multiple_of(row, rows), rows), :],
                b[pl.ds(col, cols), :],
                (((1,), (1,)), ((), ())),
                preferred_element_type=jnp.float32,
            )
            prod[pl.ds(w0, rows // OWN), :, pl.ds(col, cols)] = part.astype(jnp.bfloat16).reshape(rows // OWN, OWN, cols)

    def push(source, w, sender):
        @pl.when(w == v)
        def _():
            pltpu.make_async_copy(source, recv.at[sender], self_sem).start()

        @pl.when(w != v)
        def _():
            pltpu.make_async_remote_copy(
                src_ref=source,
                dst_ref=recv.at[sender],
                send_sem=send_sem,
                recv_sem=recv_sem,
                device_id=(w, g),
                device_id_type=MESH,
            ).start()

    def near(q):
        @pl.loop(0, 2)
        def _(t):
            w = q * 4 + xh * 2 + lax.rem(c + t + 1, 2)
            push(prod.at[w], w, v)

    def across(q):
        return pltpu.make_async_remote_copy(
            src_ref=prod.at[pl.ds(q * 4 + 2 - xh * 2, 2)],
            dst_ref=stage.at[pl.ds(q * 2, 2)],
            send_sem=x_send.at[q],
            recv_sem=x_recv.at[q],
            device_id=(flip, g),
            device_id_type=MESH,
        )

    def forward(q):
        across(q).wait_recv()

        @pl.loop(0, 2)
        def _(t):
            core = lax.rem(c + t + 1, 2)
            push(stage.at[q * 2 + core], q * 4 + xh * 2 + core, flip)

    def crossing(k):
        i = k // 2
        half = jnp.where(lax.rem(k, 2) == 0, g, h)
        n = lax.rem(i, 4)
        dy = jnp.where(n == 0, 2, jnp.where(n == 1, 1, jnp.where(n == 2, 3, 0)))
        return (2 * half + lax.rem(z + 1 + i // 4, 2)) * 4 + lax.rem(y + turn * dy + 4, 4)

    @pl.loop(0, 2)
    def _(i):
        zz = 2 * g + lax.rem(z + i, 2)
        multiply(zz * 512, zz * 16, 512, 768)

        @pl.loop(0, 4)
        def _(j):
            near(zz * 4 + lax.rem(y + turn * j + 4, 4))

    @pl.loop(0, HALF // CHUNK)
    def _(i):
        q = (2 * h + lax.rem(i + z, 2)) * 4 + lax.rem(y + turn * (i // 2) + 4, 4)
        here = a.at[pl.ds(q * CHUNK, CHUNK)]
        pltpu.make_async_remote_copy(here, here, give_sem, get_sem.at[q - 8 * h], device_id=(v, h), device_id_type=MESH).wait_recv()
        multiply(q * CHUNK, q * 4, CHUNK, ROWS)
        near(q)

        @pl.when(i == 6)
        def _():
            across(crossing(0)).start()

    @pl.loop(1, WINDOW)
    def _(k):
        across(crossing(k)).start()

    @pl.loop(0, 16)
    def _(k):
        forward(crossing(k))

        @pl.when(k + WINDOW < 16)
        def _():
            across(crossing(k + WINDOW)).start()

    for j in range(n_chunks):
        for copy in gives(j):
            copy.wait_send()

    @pl.loop(0, 16)
    def _(q):
        across(q).wait_send()

    pltpu.make_async_copy(prod.at[pl.ds(0, 2)], recv.at[pl.ds(0, 2)], self_sem).wait()
    rest = pltpu.make_async_remote_copy(
        src_ref=prod.at[pl.ds(0, N_VV - 2)],
        dst_ref=recv.at[pl.ds(0, N_VV - 2)],
        send_sem=send_sem,
        recv_sem=recv_sem,
        device_id=(flip, g),
        device_id_type=MESH,
    )
    rest.wait_send()
    rest.wait_recv()


def ladder(own, other, integrals):
    hbm = pl.BlockSpec(memory_space=pl.ANY)
    return pl.pallas_call(
        ladder_kernel,
        name="ladder",
        out_shape=pltpu.VMEM((N_VV, OWN, ROWS), jnp.bfloat16),
        in_specs=[hbm] * 3,
        out_specs=pl.BlockSpec(memory_space=pltpu.VMEM),
        scratch_shapes=[
            pltpu.VMEM((IJ, KP), jnp.bfloat16),
            pltpu.VMEM((ROWS, KP), jnp.bfloat16),
            pltpu.VMEM((N_VV, OWN, ROWS), jnp.bfloat16),
            pltpu.VMEM((N_VV // 2, OWN, ROWS), jnp.bfloat16),
            pltpu.SemaphoreType.DMA((2,)),
            pltpu.SemaphoreType.DMA,
            pltpu.SemaphoreType.DMA((HALF // CHUNK,)),
            pltpu.SemaphoreType.DMA,
            pltpu.SemaphoreType.DMA,
            pltpu.SemaphoreType.DMA,
            pltpu.SemaphoreType.DMA((16,)),
            pltpu.SemaphoreType.DMA((16,)),
        ],
        compiler_params=pltpu.CompilerParams(
            collective_id=0, has_side_effects=True, vmem_limit_bytes=40 * MIB
        ),
        cost_estimate=pl.CostEstimate(flops=2 * IJ * ROWS * KP, bytes_accessed=40 * MIB, transcendentals=0),
    )(own, other, integrals)


TCOL = 768


def swap_kernel(x, out, buf, sem):
    row = lax.broadcasted_iota(jnp.int32, (256, 256), 0)
    col = lax.broadcasted_iota(jnp.int32, (256, 256), 1)
    perm = jnp.where(lax.rem(row, 16) * 16 + row // 16 == col, 1.0, 0.0).astype(jnp.bfloat16)

    def result(i, n):
        part = (pl.ds(i * 16, 16), slice(None), pl.ds(n * TCOL, TCOL))
        return pltpu.make_async_copy(buf.at[part], out.at[part], sem.at[i, n])

    for i in range(OWN // 16):
        for n in range(ROWS // TCOL):
            for s in range(N_VV // 16):
                block = x[pl.ds(s * 16, 16), pl.ds(i * 16, 16), pl.ds(n * TCOL, TCOL)].reshape(256, TCOL)
                part = jnp.dot(perm, block, preferred_element_type=jnp.float32)
                buf[pl.ds(i * 16, 16), pl.ds(s * 16, 16), pl.ds(n * TCOL, TCOL)] = part.astype(jnp.bfloat16).reshape(16, 16, TCOL)
            result(i, n).start()
    for i in range(OWN // 16):
        for n in range(ROWS // TCOL):
            result(i, n).wait()


def swap(x):
    return pl.pallas_call(
        swap_kernel,
        name="swap",
        out_shape=jax.ShapeDtypeStruct((OWN, N_VV, ROWS), jnp.bfloat16),
        in_specs=[pl.BlockSpec(memory_space=pltpu.VMEM)],
        out_specs=pl.BlockSpec(memory_space=pl.ANY),
        scratch_shapes=[
            pltpu.VMEM((OWN, N_VV, ROWS), jnp.bfloat16),
            pltpu.SemaphoreType.DMA((OWN // 16, ROWS // TCOL)),
        ],
        compiler_params=pltpu.CompilerParams(vmem_limit_bytes=24 * MIB),
        cost_estimate=pl.CostEstimate(flops=0, bytes_accessed=2 * IJ * ROWS * 2, transcendentals=0),
    )(x)


def shards(integrals, amplitudes, orbital_irrep, pair_irrep, panel_block):
    flipped = [(i, i ^ 2) for i in range(N_VV)]
    other_irrep = lax.ppermute(pair_irrep, "vv", flipped)
    own = slice_block(0, HALF, orbital_irrep, pair_irrep, panel_block, amplitudes)
    other = slice_block(HALF // 2, HALF // 2, orbital_irrep, other_irrep, panel_block, amplitudes)
    return swap(ladder(own, other, integrals))


def solution(mesh):
    return jax.shard_map(
        shards,
        mesh=mesh,
        in_specs=(P("vv", "grp", None), P("grp", None), P(), P("vv"), P()),
        out_specs=P("vv", None, "grp"),
        check_vma=False,
    )
```

```python
import functools

import jax
import jax.numpy as jnp
from jax import lax
from jax.experimental import pallas as pl
from jax.experimental.pallas import tpu as pltpu
from jax.sharding import PartitionSpec as P

NIRR = 8
BS = 96
DW = 16
NV = NIRR * BS
KP = DW * BS
ROWS = 2304
IJ = 2048
HALF = IJ // 2
N_VV = 64
OWN = IJ // N_VV
CHUNK = 128
WINDOW = 3
MESH = pl.DeviceIdType.MESH
PART = HALF // 2
SUB_ROWS = 256
MIB = 1024 * 1024


def slice_kernel(labels, pair, other_pair, panel, amp, own, other, win, buf, in_sem, out_sem):
    panel_irrep = labels[panel[0] * BS]

    def place(irrep):
        target = irrep ^ panel_irrep
        allowed = jnp.int32(0)
        for k in range(NIRR):
            allowed += jnp.where(labels[k * BS] == target, jnp.int32(k), jnp.int32(0))
        tile = jnp.minimum(allowed * BS // 128, 4)
        return tile, allowed * BS - tile * 128

    mine, theirs = place(pair[0]), place(other_pair[0])
    parts = [(mine, 0, own, 0), (theirs, HALF // 2, other, 0), (mine, HALF // 2, own, HALF // 2)]
    units = [(p, q) for p in range(3) for q in range(DW // 4)]

    def window(p, q, j):
        (tile, _), row, _, _ = parts[p]
        d = q * 4 + j
        return pltpu.make_async_copy(
            amp.at[pl.ds(row, PART), pl.ds(pl.multiple_of(d * NV + tile * 128, 128), 256)],
            win.at[d, pl.ds(p * PART, PART)],
            in_sem.at[p, q],
        )

    def result(p, q):
        _, _, out, row = parts[p]
        cols = pl.ds(q * 4 * BS, 4 * BS)
        return pltpu.make_async_copy(buf.at[pl.ds(p * PART, PART), cols], out.at[pl.ds(row, PART), cols], out_sem.at[p, q])

    for p, q in units:
        for j in range(4):
            window(p, q, j).start()
    lane = lax.broadcasted_iota(jnp.int32, (SUB_ROWS, 128), 1)

    for p, q in units:
        off = parts[p][0][1]
        for j in range(4):
            window(p, q, j).wait()

        @pl.loop(0, PART // SUB_ROWS)
        def _(r):
            rows = pl.ds(pl.multiple_of(p * PART + r * SUB_ROWS, SUB_ROWS), SUB_ROWS)
            w = [
                pltpu.roll(win[q * 4 + j, rows].astype(jnp.float32), lax.rem((96 * j) % 128 - off + 512, 256), 1)
                for j in range(4)
            ]
            t0 = jnp.where(lane < 96, w[0][:, :128], w[1][:, :128])
            t1 = jnp.where(lane < 64, w[1][:, 128:], w[2][:, :128])
            t2 = jnp.where(lane < 32, w[2][:, 128:], w[3][:, :128])
            buf[rows, q * 384 : (q + 1) * 384] = jnp.concatenate([t0, t1, t2], axis=1).astype(jnp.bfloat16)

        result(p, q).start()
    for p, q in units:
        result(p, q).wait()


def slice_blocks(orb, pair, other_pair, panel, amp):
    smem = pl.BlockSpec(memory_space=pltpu.SMEM)
    hbm = pl.BlockSpec(memory_space=pl.ANY)
    return pl.pallas_call(
        slice_kernel,
        name="slice_blocks",
        out_shape=(jax.ShapeDtypeStruct((HALF, KP), jnp.bfloat16), jax.ShapeDtypeStruct((HALF // 2, KP), jnp.bfloat16)),
        in_specs=[smem, smem, smem, smem, hbm],
        out_specs=(hbm, hbm),
        scratch_shapes=[
            pltpu.VMEM((DW, 3 * PART, 256), jnp.bfloat16),
            pltpu.VMEM((3 * PART, KP), jnp.bfloat16),
            pltpu.SemaphoreType.DMA((3, DW // 4)),
            pltpu.SemaphoreType.DMA((3, DW // 4)),
        ],
        compiler_params=pltpu.CompilerParams(vmem_limit_bytes=44 * MIB),
        cost_estimate=pl.CostEstimate(flops=0, bytes_accessed=3 * PART * 11264, transcendentals=0),
    )(orb, pair, other_pair, panel, amp)


def ladder_kernel(own, other, integrals, recv, a, b, prod, stage, load_sem, give_sem, get_sem, send_sem, recv_sem, self_sem, x_send, x_recv):
    v = lax.axis_index("vv")
    g = lax.axis_index("grp")
    h = 1 - g
    z, y = v // 16, lax.rem(v // 4, 4)
    xh, c = lax.rem(v // 2, 2), lax.rem(v, 2)
    flip = v + 2 - 4 * xh
    turn = 1 - 2 * c
    load_b = pltpu.make_async_copy(integrals.at[0], b, load_sem.at[0])
    load_a = pltpu.make_async_copy(own, a.at[pl.ds(g * HALF, HALF)], load_sem.at[1])
    load_a.start()
    load_b.start()

    barrier = pltpu.get_barrier_semaphore()

    def greet(w, group):
        pl.semaphore_signal(barrier, inc=1, device_id=(w, group), device_id_type=MESH)

    greet(flip, g)
    greet(v, h)
    greet(flip, h)

    @pl.loop(1, N_VV // 2)
    def _(k):
        p = lax.rem(v // 4 * 2 + c + k, N_VV // 2)
        greet(p // 2 * 4 + xh * 2 + lax.rem(p, 2), g)

    pl.semaphore_wait(barrier, N_VV // 2 + 2)

    n_chunks = HALF // 2 // CHUNK

    def gives(j):
        first = pltpu.make_async_remote_copy(
            src_ref=own.at[pl.ds(j * CHUNK, CHUNK)],
            dst_ref=a.at[pl.ds(g * HALF + j * CHUNK, CHUNK)],
            send_sem=give_sem,
            recv_sem=get_sem.at[j],
            device_id=(v, h),
            device_id_type=MESH,
        )
        second = pltpu.make_async_remote_copy(
            src_ref=other.at[pl.ds(j * CHUNK, CHUNK)],
            dst_ref=a.at[pl.ds(g * HALF + HALF // 2 + j * CHUNK, CHUNK)],
            send_sem=give_sem,
            recv_sem=get_sem.at[n_chunks + j],
            device_id=(flip, h),
            device_id_type=MESH,
        )
        return first, second

    for j in range(n_chunks):
        for copy in gives(lax.rem(y + turn * j + 4, 4)):
            copy.start()
    load_a.wait()
    load_b.wait()

    def multiply(row, w0, rows, cols):
        @pl.loop(0, ROWS // cols)
        def _(n):
            col = pl.multiple_of(n * cols, cols)
            part = lax.dot_general(
                a[pl.ds(pl.multiple_of(row, rows), rows), :],
                b[pl.ds(col, cols), :],
                (((1,), (1,)), ((), ())),
                preferred_element_type=jnp.float32,
            )
            prod[pl.ds(w0, rows // OWN), :, pl.ds(col, cols)] = part.astype(jnp.bfloat16).reshape(rows // OWN, OWN, cols)

    def push(source, w, sender):
        @pl.when(w == v)
        def _():
            pltpu.make_async_copy(source, recv.at[sender], self_sem).start()

        @pl.when(w != v)
        def _():
            pltpu.make_async_remote_copy(
                src_ref=source,
                dst_ref=recv.at[sender],
                send_sem=send_sem,
                recv_sem=recv_sem,
                device_id=(w, g),
                device_id_type=MESH,
            ).start()

    def near(q):
        @pl.loop(0, 2)
        def _(t):
            w = q * 4 + xh * 2 + lax.rem(c + t + 1, 2)
            push(prod.at[w], w, v)

    def across(q):
        return pltpu.make_async_remote_copy(
            src_ref=prod.at[pl.ds(q * 4 + 2 - xh * 2, 2)],
            dst_ref=stage.at[pl.ds(q * 2, 2)],
            send_sem=x_send.at[q],
            recv_sem=x_recv.at[q],
            device_id=(flip, g),
            device_id_type=MESH,
        )

    def forward(q):
        across(q).wait_recv()

        @pl.loop(0, 2)
        def _(t):
            core = lax.rem(c + t + 1, 2)
            push(stage.at[q * 2 + core], q * 4 + xh * 2 + core, flip)

    def crossing(k):
        i = k // 2
        half = lax.rem(z // 2 + k + 1, 2)
        n = lax.rem(i, 4)
        dy = jnp.where(n == 0, 2, jnp.where(n == 1, 1, jnp.where(n == 2, 3, 0)))
        return (2 * half + lax.rem(z + 1 + i // 4, 2)) * 4 + lax.rem(y + turn * dy + 4, 4)

    @pl.loop(0, 2)
    def _(i):
        zz = 2 * g + lax.rem(z + i, 2)
        multiply(zz * 512, zz * 16, 512, 768)

        @pl.loop(0, 4)
        def _(j):
            near(zz * 4 + lax.rem(y + turn * j + 4, 4))

    @pl.loop(0, HALF // CHUNK)
    def _(i):
        q = (2 * h + lax.rem(i + z, 2)) * 4 + lax.rem(y + turn * (i // 2) + 4, 4)
        here = a.at[pl.ds(q * CHUNK, CHUNK)]
        pltpu.make_async_remote_copy(here, here, give_sem, get_sem.at[q - 8 * h], device_id=(v, h), device_id_type=MESH).wait_recv()
        multiply(q * CHUNK, q * 4, CHUNK, ROWS)
        near(q)

        @pl.when(i == 6)
        def _():
            across(crossing(0)).start()

    @pl.loop(1, WINDOW)
    def _(k):
        across(crossing(k)).start()

    @pl.loop(0, 16)
    def _(k):
        forward(crossing(k))

        @pl.when(k + WINDOW < 16)
        def _():
            across(crossing(k + WINDOW)).start()

    for j in range(n_chunks):
        for copy in gives(j):
            copy.wait_send()

    @pl.loop(0, 16)
    def _(q):
        across(q).wait_send()

    pltpu.make_async_copy(prod.at[pl.ds(0, 2)], recv.at[pl.ds(0, 2)], self_sem).wait()
    rest = pltpu.make_async_remote_copy(
        src_ref=prod.at[pl.ds(0, N_VV - 2)],
        dst_ref=recv.at[pl.ds(0, N_VV - 2)],
        send_sem=send_sem,
        recv_sem=recv_sem,
        device_id=(flip, g),
        device_id_type=MESH,
    )
    rest.wait_send()
    rest.wait_recv()


def ladder(own, other, integrals):
    hbm = pl.BlockSpec(memory_space=pl.ANY)
    return pl.pallas_call(
        ladder_kernel,
        name="ladder",
        out_shape=pltpu.VMEM((N_VV, OWN, ROWS), jnp.bfloat16),
        in_specs=[hbm] * 3,
        out_specs=pl.BlockSpec(memory_space=pltpu.VMEM),
        scratch_shapes=[
            pltpu.VMEM((IJ, KP), jnp.bfloat16),
            pltpu.VMEM((ROWS, KP), jnp.bfloat16),
            pltpu.VMEM((N_VV, OWN, ROWS), jnp.bfloat16),
            pltpu.VMEM((N_VV // 2, OWN, ROWS), jnp.bfloat16),
            pltpu.SemaphoreType.DMA((2,)),
            pltpu.SemaphoreType.DMA,
            pltpu.SemaphoreType.DMA((HALF // CHUNK,)),
            pltpu.SemaphoreType.DMA,
            pltpu.SemaphoreType.DMA,
            pltpu.SemaphoreType.DMA,
            pltpu.SemaphoreType.DMA((16,)),
            pltpu.SemaphoreType.DMA((16,)),
        ],
        compiler_params=pltpu.CompilerParams(
            collective_id=0, has_side_effects=True, vmem_limit_bytes=40 * MIB
        ),
        cost_estimate=pl.CostEstimate(flops=2 * IJ * ROWS * KP, bytes_accessed=40 * MIB, transcendentals=0),
    )(own, other, integrals)


TCOL = 768


def swap_kernel(x, out, buf, sem):
    row = lax.broadcasted_iota(jnp.int32, (256, 256), 0)
    col = lax.broadcasted_iota(jnp.int32, (256, 256), 1)
    perm = jnp.where(lax.rem(row, 16) * 16 + row // 16 == col, 1.0, 0.0).astype(jnp.bfloat16)

    def result(i, n):
        part = (pl.ds(i * 16, 16), slice(None), pl.ds(n * TCOL, TCOL))
        return pltpu.make_async_copy(buf.at[part], out.at[part], sem.at[i, n])

    for i in range(OWN // 16):
        for n in range(ROWS // TCOL):
            for s in range(N_VV // 16):
                block = x[pl.ds(s * 16, 16), pl.ds(i * 16, 16), pl.ds(n * TCOL, TCOL)].reshape(256, TCOL)
                part = jnp.dot(perm, block, preferred_element_type=jnp.float32)
                buf[pl.ds(i * 16, 16), pl.ds(s * 16, 16), pl.ds(n * TCOL, TCOL)] = part.astype(jnp.bfloat16).reshape(16, 16, TCOL)
            result(i, n).start()
    for i in range(OWN // 16):
        for n in range(ROWS // TCOL):
            result(i, n).wait()


def swap(x):
    return pl.pallas_call(
        swap_kernel,
        name="swap",
        out_shape=jax.ShapeDtypeStruct((OWN, N_VV, ROWS), jnp.bfloat16),
        in_specs=[pl.BlockSpec(memory_space=pltpu.VMEM)],
        out_specs=pl.BlockSpec(memory_space=pl.ANY),
        scratch_shapes=[
            pltpu.VMEM((OWN, N_VV, ROWS), jnp.bfloat16),
            pltpu.SemaphoreType.DMA((OWN // 16, ROWS // TCOL)),
        ],
        compiler_params=pltpu.CompilerParams(vmem_limit_bytes=24 * MIB),
        cost_estimate=pl.CostEstimate(flops=0, bytes_accessed=2 * IJ * ROWS * 2, transcendentals=0),
    )(x)


def shards(integrals, amplitudes, orbital_irrep, pair_irrep, panel_block):
    flipped = [(i, i ^ 2) for i in range(N_VV)]
    other_irrep = lax.ppermute(pair_irrep, "vv", flipped)
    own, other = slice_blocks(orbital_irrep, pair_irrep, other_irrep, panel_block, amplitudes)
    return swap(ladder(own, other, integrals))


def solution(mesh):
    return jax.shard_map(
        shards,
        mesh=mesh,
        in_specs=(P("vv", "grp", None), P("grp", None), P(), P("vv"), P()),
        out_specs=P("vv", None, "grp"),
        check_vma=False,
    )
```

```python
import functools

import jax
import jax.numpy as jnp
from jax import lax
from jax.experimental import pallas as pl
from jax.experimental.pallas import tpu as pltpu
from jax.sharding import PartitionSpec as P

NIRR = 8
BS = 96
DW = 16
NV = NIRR * BS
KP = DW * BS
ROWS = 2304
IJ = 2048
HALF = IJ // 2
N_VV = 64
OWN = IJ // N_VV
CHUNK = 128
WINDOW = 4
CROSS = N_VV // 2
MESH = pl.DeviceIdType.MESH
PART = HALF // 2
SUB_ROWS = 256
MIB = 1024 * 1024


def slice_kernel(labels, pair, other_pair, panel, amp, own, other, win, buf, in_sem, out_sem):
    panel_irrep = labels[panel[0] * BS]

    def place(irrep):
        target = irrep ^ panel_irrep
        allowed = jnp.int32(0)
        for k in range(NIRR):
            allowed += jnp.where(labels[k * BS] == target, jnp.int32(k), jnp.int32(0))
        tile = jnp.minimum(allowed * BS // 128, 4)
        return tile, allowed * BS - tile * 128

    mine, theirs = place(pair[0]), place(other_pair[0])
    parts = [(mine, 0, own, 0), (theirs, HALF // 2, other, 0), (mine, HALF // 2, own, HALF // 2)]
    units = [(p, q) for p in range(3) for q in range(DW // 4)]

    def window(p, q, j):
        (tile, _), row, _, _ = parts[p]
        d = q * 4 + j
        return pltpu.make_async_copy(
            amp.at[pl.ds(row, PART), pl.ds(pl.multiple_of(d * NV + tile * 128, 128), 256)],
            win.at[d, pl.ds(p * PART, PART)],
            in_sem.at[p, q],
        )

    def result(p, q):
        _, _, out, row = parts[p]
        cols = pl.ds(q * 4 * BS, 4 * BS)
        return pltpu.make_async_copy(buf.at[pl.ds(p * PART, PART), cols], out.at[pl.ds(row, PART), cols], out_sem.at[p, q])

    for p, q in units:
        for j in range(4):
            window(p, q, j).start()
    lane = lax.broadcasted_iota(jnp.int32, (SUB_ROWS, 128), 1)

    for p, q in units:
        off = parts[p][0][1]
        for j in range(4):
            window(p, q, j).wait()

        @pl.loop(0, PART // SUB_ROWS)
        def _(r):
            rows = pl.ds(pl.multiple_of(p * PART + r * SUB_ROWS, SUB_ROWS), SUB_ROWS)
            w = [
                pltpu.roll(win[q * 4 + j, rows].astype(jnp.float32), lax.rem((96 * j) % 128 - off + 512, 256), 1)
                for j in range(4)
            ]
            t0 = jnp.where(lane < 96, w[0][:, :128], w[1][:, :128])
            t1 = jnp.where(lane < 64, w[1][:, 128:], w[2][:, :128])
            t2 = jnp.where(lane < 32, w[2][:, 128:], w[3][:, :128])
            buf[rows, q * 384 : (q + 1) * 384] = jnp.concatenate([t0, t1, t2], axis=1).astype(jnp.bfloat16)

        result(p, q).start()
    for p, q in units:
        result(p, q).wait()


def slice_blocks(orb, pair, other_pair, panel, amp):
    smem = pl.BlockSpec(memory_space=pltpu.SMEM)
    hbm = pl.BlockSpec(memory_space=pl.ANY)
    return pl.pallas_call(
        slice_kernel,
        name="slice_blocks",
        out_shape=(jax.ShapeDtypeStruct((HALF, KP), jnp.bfloat16), jax.ShapeDtypeStruct((HALF // 2, KP), jnp.bfloat16)),
        in_specs=[smem, smem, smem, smem, hbm],
        out_specs=(hbm, hbm),
        scratch_shapes=[
            pltpu.VMEM((DW, 3 * PART, 256), jnp.bfloat16),
            pltpu.VMEM((3 * PART, KP), jnp.bfloat16),
            pltpu.SemaphoreType.DMA((3, DW // 4)),
            pltpu.SemaphoreType.DMA((3, DW // 4)),
        ],
        compiler_params=pltpu.CompilerParams(vmem_limit_bytes=44 * MIB),
        cost_estimate=pl.CostEstimate(flops=0, bytes_accessed=3 * PART * 11264, transcendentals=0),
    )(orb, pair, other_pair, panel, amp)


def ladder_kernel(own, other, integrals, recv, a, b, prod, stage, load_sem, give_sem, get_sem, send_sem, recv_sem, self_sem, x_send, x_recv):
    v = lax.axis_index("vv")
    g = lax.axis_index("grp")
    h = 1 - g
    z, y = v // 16, lax.rem(v // 4, 4)
    xh, c = lax.rem(v // 2, 2), lax.rem(v, 2)
    flip = v + 2 - 4 * xh
    turn = 1 - 2 * c
    load_b = pltpu.make_async_copy(integrals.at[0], b, load_sem.at[0])
    load_a = pltpu.make_async_copy(own, a.at[pl.ds(g * HALF, HALF)], load_sem.at[1])
    load_a.start()
    load_b.start()

    barrier = pltpu.get_barrier_semaphore()

    def greet(w, group):
        pl.semaphore_signal(barrier, inc=1, device_id=(w, group), device_id_type=MESH)

    greet(flip, g)
    greet(v, h)
    greet(flip, h)

    @pl.loop(1, N_VV // 2)
    def _(k):
        p = lax.rem(v // 4 * 2 + c + k, N_VV // 2)
        greet(p // 2 * 4 + xh * 2 + lax.rem(p, 2), g)

    pl.semaphore_wait(barrier, N_VV // 2 + 2)

    n_chunks = HALF // 2 // CHUNK

    def gives(j):
        first = pltpu.make_async_remote_copy(
            src_ref=own.at[pl.ds(j * CHUNK, CHUNK)],
            dst_ref=a.at[pl.ds(g * HALF + j * CHUNK, CHUNK)],
            send_sem=give_sem,
            recv_sem=get_sem.at[j],
            device_id=(v, h),
            device_id_type=MESH,
        )
        second = pltpu.make_async_remote_copy(
            src_ref=other.at[pl.ds(j * CHUNK, CHUNK)],
            dst_ref=a.at[pl.ds(g * HALF + HALF // 2 + j * CHUNK, CHUNK)],
            send_sem=give_sem,
            recv_sem=get_sem.at[n_chunks + j],
            device_id=(flip, h),
            device_id_type=MESH,
        )
        return first, second

    for j in range(n_chunks):
        for copy in gives(lax.rem(y + turn * j + 4, 4)):
            copy.start()
    load_a.wait()
    load_b.wait()

    def multiply(row, w0, rows, cols):
        @pl.loop(0, ROWS // cols)
        def _(n):
            col = pl.multiple_of(n * cols, cols)
            part = lax.dot_general(
                a[pl.ds(pl.multiple_of(row, rows), rows), :],
                b[pl.ds(col, cols), :],
                (((1,), (1,)), ((), ())),
                preferred_element_type=jnp.float32,
            )
            prod[pl.ds(w0, rows // OWN), :, pl.ds(col, cols)] = part.astype(jnp.bfloat16).reshape(rows // OWN, OWN, cols)

    def push(source, w, sender):
        @pl.when(w == v)
        def _():
            pltpu.make_async_copy(source, recv.at[sender], self_sem).start()

        @pl.when(w != v)
        def _():
            pltpu.make_async_remote_copy(
                src_ref=source,
                dst_ref=recv.at[sender],
                send_sem=send_sem,
                recv_sem=recv_sem,
                device_id=(w, g),
                device_id_type=MESH,
            ).start()

    def near(q):
        @pl.loop(0, 2)
        def _(t):
            w = q * 4 + xh * 2 + lax.rem(c + t + 1, 2)
            push(prod.at[w], w, v)

    def crossing(k):
        i = k // 2
        half = lax.rem(z // 2 + k + 1, 2)
        n = lax.rem(i, 4)
        dy = jnp.where(n == 0, 2, jnp.where(n == 1, 1, jnp.where(n == 2, 3, 0)))
        return (2 * half + lax.rem(z + 1 + i // 4, 2)) * 4 + lax.rem(y + turn * dy + 4, 4)

    def across(u):
        q, core = crossing(u // 2), lax.rem(c + u + 1, 2)
        return pltpu.make_async_remote_copy(
            src_ref=prod.at[q * 4 + 2 - xh * 2 + core],
            dst_ref=stage.at[q * 2 + core],
            send_sem=x_send.at[u],
            recv_sem=x_recv.at[u],
            device_id=(flip, g),
            device_id_type=MESH,
        )

    def forward(u):
        across(u).wait_recv()
        q, core = crossing(u // 2), lax.rem(c + u + 1, 2)
        push(stage.at[q * 2 + core], q * 4 + xh * 2 + core, flip)

    @pl.loop(0, 2)
    def _(i):
        zz = 2 * g + lax.rem(z + i, 2)
        multiply(zz * 512, zz * 16, 512, 768)

        @pl.loop(0, 4)
        def _(j):
            near(zz * 4 + lax.rem(y + turn * j + 4, 4))

    @pl.loop(0, HALF // CHUNK)
    def _(i):
        q = (2 * h + lax.rem(i + z, 2)) * 4 + lax.rem(y + turn * (i // 2) + 4, 4)
        here = a.at[pl.ds(q * CHUNK, CHUNK)]
        pltpu.make_async_remote_copy(here, here, give_sem, get_sem.at[q - 8 * h], device_id=(v, h), device_id_type=MESH).wait_recv()
        multiply(q * CHUNK, q * 4, CHUNK, ROWS)
        near(q)

        @pl.when(i == 6)
        def _():
            across(0).start()
            across(1).start()

    @pl.loop(2, WINDOW)
    def _(u):
        across(u).start()

    @pl.loop(0, CROSS)
    def _(u):
        forward(u)

        @pl.when(u + WINDOW < CROSS)
        def _():
            across(u + WINDOW).start()

    for j in range(n_chunks):
        for copy in gives(j):
            copy.wait_send()

    @pl.loop(0, CROSS)
    def _(u):
        across(u).wait_send()

    pltpu.make_async_copy(prod.at[pl.ds(0, 2)], recv.at[pl.ds(0, 2)], self_sem).wait()
    rest = pltpu.make_async_remote_copy(
        src_ref=prod.at[pl.ds(0, N_VV - 2)],
        dst_ref=recv.at[pl.ds(0, N_VV - 2)],
        send_sem=send_sem,
        recv_sem=recv_sem,
        device_id=(flip, g),
        device_id_type=MESH,
    )
    rest.wait_send()
    rest.wait_recv()


def ladder(own, other, integrals):
    hbm = pl.BlockSpec(memory_space=pl.ANY)
    return pl.pallas_call(
        ladder_kernel,
        name="ladder",
        out_shape=pltpu.VMEM((N_VV, OWN, ROWS), jnp.bfloat16),
        in_specs=[hbm] * 3,
        out_specs=pl.BlockSpec(memory_space=pltpu.VMEM),
        scratch_shapes=[
            pltpu.VMEM((IJ, KP), jnp.bfloat16),
            pltpu.VMEM((ROWS, KP), jnp.bfloat16),
            pltpu.VMEM((N_VV, OWN, ROWS), jnp.bfloat16),
            pltpu.VMEM((N_VV // 2, OWN, ROWS), jnp.bfloat16),
            pltpu.SemaphoreType.DMA((2,)),
            pltpu.SemaphoreType.DMA,
            pltpu.SemaphoreType.DMA((HALF // CHUNK,)),
            pltpu.SemaphoreType.DMA,
            pltpu.SemaphoreType.DMA,
            pltpu.SemaphoreType.DMA,
            pltpu.SemaphoreType.DMA((CROSS,)),
            pltpu.SemaphoreType.DMA((CROSS,)),
        ],
        compiler_params=pltpu.CompilerParams(
            collective_id=0, has_side_effects=True, vmem_limit_bytes=40 * MIB
        ),
        cost_estimate=pl.CostEstimate(flops=2 * IJ * ROWS * KP, bytes_accessed=40 * MIB, transcendentals=0),
    )(own, other, integrals)


TCOL = 768


def swap_kernel(x, out, buf, sem):
    row = lax.broadcasted_iota(jnp.int32, (256, 256), 0)
    col = lax.broadcasted_iota(jnp.int32, (256, 256), 1)
    perm = jnp.where(lax.rem(row, 16) * 16 + row // 16 == col, 1.0, 0.0).astype(jnp.bfloat16)

    def result(i, n):
        part = (pl.ds(i * 16, 16), slice(None), pl.ds(n * TCOL, TCOL))
        return pltpu.make_async_copy(buf.at[part], out.at[part], sem.at[i, n])

    for i in range(OWN // 16):
        for n in range(ROWS // TCOL):
            for s in range(N_VV // 16):
                block = x[pl.ds(s * 16, 16), pl.ds(i * 16, 16), pl.ds(n * TCOL, TCOL)].reshape(256, TCOL)
                part = jnp.dot(perm, block, preferred_element_type=jnp.float32)
                buf[pl.ds(i * 16, 16), pl.ds(s * 16, 16), pl.ds(n * TCOL, TCOL)] = part.astype(jnp.bfloat16).reshape(16, 16, TCOL)
            result(i, n).start()
    for i in range(OWN // 16):
        for n in range(ROWS // TCOL):
            result(i, n).wait()


def swap(x):
    return pl.pallas_call(
        swap_kernel,
        name="swap",
        out_shape=jax.ShapeDtypeStruct((OWN, N_VV, ROWS), jnp.bfloat16),
        in_specs=[pl.BlockSpec(memory_space=pltpu.VMEM)],
        out_specs=pl.BlockSpec(memory_space=pl.ANY),
        scratch_shapes=[
            pltpu.VMEM((OWN, N_VV, ROWS), jnp.bfloat16),
            pltpu.SemaphoreType.DMA((OWN // 16, ROWS // TCOL)),
        ],
        compiler_params=pltpu.CompilerParams(vmem_limit_bytes=24 * MIB),
        cost_estimate=pl.CostEstimate(flops=0, bytes_accessed=2 * IJ * ROWS * 2, transcendentals=0),
    )(x)


def shards(integrals, amplitudes, orbital_irrep, pair_irrep, panel_block):
    flipped = [(i, i ^ 2) for i in range(N_VV)]
    other_irrep = lax.ppermute(pair_irrep, "vv", flipped)
    own, other = slice_blocks(orbital_irrep, pair_irrep, other_irrep, panel_block, amplitudes)
    return swap(ladder(own, other, integrals))


def solution(mesh):
    return jax.shard_map(
        shards,
        mesh=mesh,
        in_specs=(P("vv", "grp", None), P("grp", None), P(), P("vv"), P()),
        out_specs=P("vv", None, "grp"),
        check_vma=False,
    )
```

```python
import functools

import jax
import jax.numpy as jnp
from jax import lax
from jax.experimental import pallas as pl
from jax.experimental.pallas import tpu as pltpu
from jax.sharding import PartitionSpec as P

NIRR = 8
BS = 96
DW = 16
NV = NIRR * BS
KP = DW * BS
ROWS = 2304
IJ = 2048
HALF = IJ // 2
N_VV = 64
OWN = IJ // N_VV
CHUNK = 128
WINDOW = 4
CROSS = N_VV // 2
MESH = pl.DeviceIdType.MESH
PART = HALF // 2
MIB = 1024 * 1024


def place(labels, panel, irrep):
    panel_irrep = jnp.int32(0)
    for k in range(NIRR):
        panel_irrep += jnp.where(panel == k, labels[k * BS], jnp.int32(0))
    target = irrep ^ panel_irrep
    allowed = jnp.int32(0)
    for k in range(NIRR):
        allowed += jnp.where(labels[k * BS] == target, jnp.int32(k), jnp.int32(0))
    return allowed


def choose(rows, allowed, out, row):
    lane = lax.broadcasted_iota(jnp.int32, (CHUNK, 128), 1)
    upper, rest = allowed // 4, lax.rem(allowed, 4)
    off = lax.rem(allowed * BS, 128)
    for q in range(DW // 4):
        w = []
        for j in range(4):
            start = (q * 4 + j) * NV
            t = [
                jnp.where(upper == 1, rows[:, start + 384 + n : start + 512 + n], rows[:, start + n : start + 128 + n]).astype(jnp.float32)
                for n in (0, 128, 256)
            ]
            low = jnp.where(rest < 2, t[0], jnp.where(rest == 2, t[1], t[2]))
            x = jnp.concatenate([low, jnp.where(rest < 2, t[1], t[2])], axis=1)
            shift = (96 * j) % 128
            w.append(pltpu.roll(x, lax.rem(shift - off + 256, 256), 1))
        t0 = jnp.where(lane < 96, w[0][:, :128], w[1][:, :128])
        t1 = jnp.where(lane < 64, w[1][:, 128:], w[2][:, :128])
        t2 = jnp.where(lane < 32, w[2][:, 128:], w[3][:, :128])
        out[pl.ds(row, CHUNK), q * 384 : (q + 1) * 384] = jnp.concatenate([t0, t1, t2], axis=1).astype(jnp.bfloat16)


def ladder_kernel(labels, pair, other_pair, panel, amp, integrals, recv, a, b, prod, stage, other, a0, a1, b0, b1, load_sem, row_sem, give_sem, get_sem, send_sem, recv_sem, self_sem, x_send, x_recv):
    v = lax.axis_index("vv")
    g = lax.axis_index("grp")
    h = 1 - g
    z, y = v // 16, lax.rem(v // 4, 4)
    xh, c = lax.rem(v // 2, 2), lax.rem(v, 2)
    flip = v + 2 - 4 * xh
    turn = 1 - 2 * c
    load_b = pltpu.make_async_copy(integrals.at[0], b, load_sem)
    held = ((a0, b0), (a1, b1))

    def chunk(j):
        return pl.multiple_of(lax.rem(y + turn * j + 4, 4) * CHUNK, CHUNK)

    def load(j, parity, part):
        return pltpu.make_async_copy(
            amp.at[pl.ds(part * PART + chunk(j), CHUNK)], held[parity][part], row_sem.at[parity, part]
        )

    for parity in range(2):
        for part in range(2):
            load(parity, parity, part).start()

    barrier = pltpu.get_barrier_semaphore()

    def greet(w, group):
        pl.semaphore_signal(barrier, inc=1, device_id=(w, group), device_id_type=MESH)

    greet(flip, g)
    greet(v, h)
    greet(flip, h)

    @pl.loop(1, N_VV // 2)
    def _(k):
        p = lax.rem(v // 4 * 2 + c + k, N_VV // 2)
        greet(p // 2 * 4 + xh * 2 + lax.rem(p, 2), g)

    pl.semaphore_wait(barrier, N_VV // 2 + 2)

    mine = place(labels, panel[0], pair[0])
    theirs = place(labels, panel[0], other_pair[0])

    def gives(j):
        row = chunk(j)
        here = a.at[pl.ds(g * HALF + row, CHUNK)]
        first = pltpu.make_async_remote_copy(
            src_ref=here,
            dst_ref=here,
            send_sem=give_sem,
            recv_sem=get_sem.at[row // CHUNK],
            device_id=(v, h),
            device_id_type=MESH,
        )
        second = pltpu.make_async_remote_copy(
            src_ref=other.at[pl.ds(row, CHUNK)],
            dst_ref=a.at[pl.ds(g * HALF + PART + row, CHUNK)],
            send_sem=give_sem,
            recv_sem=get_sem.at[PART // CHUNK + row // CHUNK],
            device_id=(flip, h),
            device_id_type=MESH,
        )
        return first, second

    @pl.loop(0, 2)
    def _(i):
        for parity in range(2):
            j = 2 * i + parity
            row = chunk(j)
            first, second = gives(j)
            load(j, parity, 0).wait()
            choose(held[parity][0], mine, a, pl.multiple_of(g * HALF + row, CHUNK))
            first.start()

            @pl.when(i == 0)
            def _():
                load(j + 2, parity, 0).start()

            load(j, parity, 1).wait()
            choose(held[parity][1], theirs, other, row)
            second.start()
            choose(held[parity][1], mine, a, pl.multiple_of(g * HALF + PART + row, CHUNK))

            @pl.when(i == 0)
            def _():
                load(j + 2, parity, 1).start()

        @pl.when(i == 0)
        def _():
            load_b.start()

    load_b.wait()

    def multiply(row, w0, rows, cols):
        @pl.loop(0, ROWS // cols)
        def _(n):
            col = pl.multiple_of(n * cols, cols)
            part = lax.dot_general(
                a[pl.ds(pl.multiple_of(row, rows), rows), :],
                b[pl.ds(col, cols), :],
                (((1,), (1,)), ((), ())),
                preferred_element_type=jnp.float32,
            )
            prod[pl.ds(w0, rows // OWN), :, pl.ds(col, cols)] = part.astype(jnp.bfloat16).reshape(rows // OWN, OWN, cols)

    def push(source, w, sender):
        @pl.when(w == v)
        def _():
            pltpu.make_async_copy(source, recv.at[sender], self_sem).start()

        @pl.when(w != v)
        def _():
            pltpu.make_async_remote_copy(
                src_ref=source,
                dst_ref=recv.at[sender],
                send_sem=send_sem,
                recv_sem=recv_sem,
                device_id=(w, g),
                device_id_type=MESH,
            ).start()

    def near(q):
        @pl.loop(0, 2)
        def _(t):
            w = q * 4 + xh * 2 + lax.rem(c + t + 1, 2)
            push(prod.at[w], w, v)

    def crossing(k):
        i = k // 2
        half = lax.rem(z // 2 + k + 1, 2)
        n = lax.rem(i, 4)
        dy = lax.rem(n + 1, 4)
        return (2 * half + lax.rem(z + 1 + i // 4, 2)) * 4 + lax.rem(y + turn * dy + 4, 4)

    def across(u):
        q, core = crossing(u // 2), lax.rem(c + u + 1, 2)
        return pltpu.make_async_remote_copy(
            src_ref=prod.at[q * 4 + 2 - xh * 2 + core],
            dst_ref=stage.at[q * 2 + core],
            send_sem=x_send.at[u],
            recv_sem=x_recv.at[u],
            device_id=(flip, g),
            device_id_type=MESH,
        )

    def forward(u):
        across(u).wait_recv()
        q, core = crossing(u // 2), lax.rem(c + u + 1, 2)
        push(stage.at[q * 2 + core], q * 4 + xh * 2 + core, flip)

    @pl.loop(0, 2)
    def _(i):
        zz = 2 * g + lax.rem(z + i, 2)
        multiply(zz * 512, zz * 16, 512, 768)

        @pl.loop(0, 4)
        def _(j):
            near(zz * 4 + lax.rem(y + turn * j + 4, 4))

    @pl.loop(0, HALF // CHUNK)
    def _(i):
        q = (2 * h + lax.rem(i + z, 2)) * 4 + lax.rem(y + turn * (i // 2) + 4, 4)
        here = a.at[pl.ds(q * CHUNK, CHUNK)]
        pltpu.make_async_remote_copy(here, here, give_sem, get_sem.at[q - 8 * h], device_id=(v, h), device_id_type=MESH).wait_recv()
        multiply(q * CHUNK, q * 4, CHUNK, ROWS)
        near(q)

        @pl.when(i == 4)
        def _():
            for u in range(WINDOW):
                across(u).start()

    @pl.loop(0, CROSS)
    def _(u):
        forward(u)

        @pl.when(u + WINDOW < CROSS)
        def _():
            across(u + WINDOW).start()

    for j in range(PART // CHUNK):
        for copy in gives(j):
            copy.wait_send()

    @pl.loop(0, CROSS)
    def _(u):
        across(u).wait_send()

    pltpu.make_async_copy(prod.at[pl.ds(0, 2)], recv.at[pl.ds(0, 2)], self_sem).wait()
    rest = pltpu.make_async_remote_copy(
        src_ref=prod.at[pl.ds(0, N_VV - 2)],
        dst_ref=recv.at[pl.ds(0, N_VV - 2)],
        send_sem=send_sem,
        recv_sem=recv_sem,
        device_id=(flip, g),
        device_id_type=MESH,
    )
    rest.wait_send()
    rest.wait_recv()


def ladder(labels, pair, other_pair, panel, amp, integrals):
    hbm = pl.BlockSpec(memory_space=pl.ANY)
    smem = pl.BlockSpec(memory_space=pltpu.SMEM)
    return pl.pallas_call(
        ladder_kernel,
        name="ladder",
        out_shape=pltpu.VMEM((N_VV, OWN, ROWS), jnp.bfloat16),
        in_specs=[smem] * 4 + [hbm] * 2,
        out_specs=pl.BlockSpec(memory_space=pltpu.VMEM),
        scratch_shapes=[
            pltpu.VMEM((IJ, KP), jnp.bfloat16),
            pltpu.VMEM((ROWS, KP), jnp.bfloat16),
            pltpu.VMEM((N_VV, OWN, ROWS), jnp.bfloat16),
            pltpu.VMEM((N_VV // 2, OWN, ROWS), jnp.bfloat16),
            pltpu.VMEM((PART, KP), jnp.bfloat16),
            pltpu.VMEM((CHUNK, DW * NV), jnp.bfloat16),
            pltpu.VMEM((CHUNK, DW * NV), jnp.bfloat16),
            pltpu.VMEM((CHUNK, DW * NV), jnp.bfloat16),
            pltpu.VMEM((CHUNK, DW * NV), jnp.bfloat16),
            pltpu.SemaphoreType.DMA,
            pltpu.SemaphoreType.DMA((2, 2)),
            pltpu.SemaphoreType.DMA,
            pltpu.SemaphoreType.DMA((HALF // CHUNK,)),
            pltpu.SemaphoreType.DMA,
            pltpu.SemaphoreType.DMA,
            pltpu.SemaphoreType.DMA,
            pltpu.SemaphoreType.DMA((CROSS,)),
            pltpu.SemaphoreType.DMA((CROSS,)),
        ],
        compiler_params=pltpu.CompilerParams(
            collective_id=0, has_side_effects=True, vmem_limit_bytes=48 * MIB
        ),
        cost_estimate=pl.CostEstimate(flops=2 * IJ * ROWS * KP, bytes_accessed=60 * MIB, transcendentals=0),
    )(labels, pair, other_pair, panel, amp, integrals)


TCOL = 768


def swap_kernel(x, out, buf, sem):
    row = lax.broadcasted_iota(jnp.int32, (256, 256), 0)
    col = lax.broadcasted_iota(jnp.int32, (256, 256), 1)
    perm = jnp.where(lax.rem(row, 16) * 16 + row // 16 == col, 1.0, 0.0).astype(jnp.bfloat16)

    def result(i, n):
        part = (pl.ds(i * 16, 16), slice(None), pl.ds(n * TCOL, TCOL))
        return pltpu.make_async_copy(buf.at[part], out.at[part], sem.at[i, n])

    for i in range(OWN // 16):
        for n in range(ROWS // TCOL):
            for s in range(N_VV // 16):
                block = x[pl.ds(s * 16, 16), pl.ds(i * 16, 16), pl.ds(n * TCOL, TCOL)].reshape(256, TCOL)
                part = jnp.dot(perm, block, preferred_element_type=jnp.float32)
                buf[pl.ds(i * 16, 16), pl.ds(s * 16, 16), pl.ds(n * TCOL, TCOL)] = part.astype(jnp.bfloat16).reshape(16, 16, TCOL)
            result(i, n).start()
    for i in range(OWN // 16):
        for n in range(ROWS // TCOL):
            result(i, n).wait()


def swap(x):
    return pl.pallas_call(
        swap_kernel,
        name="swap",
        out_shape=jax.ShapeDtypeStruct((OWN, N_VV, ROWS), jnp.bfloat16),
        in_specs=[pl.BlockSpec(memory_space=pltpu.VMEM)],
        out_specs=pl.BlockSpec(memory_space=pl.ANY),
        scratch_shapes=[
            pltpu.VMEM((OWN, N_VV, ROWS), jnp.bfloat16),
            pltpu.SemaphoreType.DMA((OWN // 16, ROWS // TCOL)),
        ],
        compiler_params=pltpu.CompilerParams(vmem_limit_bytes=24 * MIB),
        cost_estimate=pl.CostEstimate(flops=0, bytes_accessed=2 * IJ * ROWS * 2, transcendentals=0),
    )(x)


def shards(integrals, amplitudes, orbital_irrep, pair_irrep, panel_block):
    flipped = [(i, i ^ 2) for i in range(N_VV)]
    other_irrep = lax.ppermute(pair_irrep, "vv", flipped)
    return swap(ladder(orbital_irrep, pair_irrep, other_irrep, panel_block, amplitudes, integrals))


def solution(mesh):
    return jax.shard_map(
        shards,
        mesh=mesh,
        in_specs=(P("vv", "grp", None), P("grp", None), P(), P("vv"), P()),
        out_specs=P("vv", None, "grp"),
        check_vma=False,
    )
```

```python
import functools

import jax
import jax.numpy as jnp
from jax import lax
from jax.experimental import pallas as pl
from jax.experimental.pallas import tpu as pltpu
from jax.sharding import PartitionSpec as P

NIRR = 8
BS = 96
DW = 16
NV = NIRR * BS
KP = DW * BS
ROWS = 2304
IJ = 2048
HALF = IJ // 2
N_VV = 64
OWN = IJ // N_VV
CHUNK = 128
WINDOW = 4
CROSS = N_VV // 2
COLS = 768
MESH = pl.DeviceIdType.MESH
PART = HALF // 2
MIB = 1024 * 1024


def place(labels, panel, irrep):
    panel_irrep = jnp.int32(0)
    for k in range(NIRR):
        panel_irrep += jnp.where(panel == k, labels[k * BS], jnp.int32(0))
    target = irrep ^ panel_irrep
    allowed = jnp.int32(0)
    for k in range(NIRR):
        allowed += jnp.where(labels[k * BS] == target, jnp.int32(k), jnp.int32(0))
    return allowed


def choose(rows, allowed, out, row):
    lane = lax.broadcasted_iota(jnp.int32, (CHUNK, 128), 1)
    upper, rest = allowed // 4, lax.rem(allowed, 4)
    off = lax.rem(allowed * BS, 128)
    for q in range(DW // 4):
        w = []
        for j in range(4):
            start = (q * 4 + j) * NV
            t = [
                jnp.where(upper == 1, rows[:, start + 384 + n : start + 512 + n], rows[:, start + n : start + 128 + n]).astype(jnp.float32)
                for n in (0, 128, 256)
            ]
            low = jnp.where(rest < 2, t[0], jnp.where(rest == 2, t[1], t[2]))
            x = jnp.concatenate([low, jnp.where(rest < 2, t[1], t[2])], axis=1)
            shift = (96 * j) % 128
            w.append(pltpu.roll(x, lax.rem(shift - off + 256, 256), 1))
        t0 = jnp.where(lane < 96, w[0][:, :128], w[1][:, :128])
        t1 = jnp.where(lane < 64, w[1][:, 128:], w[2][:, :128])
        t2 = jnp.where(lane < 32, w[2][:, 128:], w[3][:, :128])
        out[pl.ds(row, CHUNK), q * 384 : (q + 1) * 384] = jnp.concatenate([t0, t1, t2], axis=1).astype(jnp.bfloat16)


def ladder_kernel(labels, pair, other_pair, panel, amp, integrals, recv, a, b, prod, stage, other, a0, a1, b0, b1, load_sem, row_sem, give_sem, get_sem, send_sem, recv_sem, self_sem, x_send, x_recv):
    v = lax.axis_index("vv")
    g = lax.axis_index("grp")
    h = 1 - g
    z, y = v // 16, lax.rem(v // 4, 4)
    xh, c = lax.rem(v // 2, 2), lax.rem(v, 2)
    flip = v + 2 - 4 * xh
    turn = 1 - 2 * c
    load_b = pltpu.make_async_copy(integrals.at[0], b, load_sem)
    held = ((a0, b0), (a1, b1))

    def chunk(j):
        return pl.multiple_of(lax.rem(y + turn * j + 4, 4) * CHUNK, CHUNK)

    def load(j, parity, part):
        return pltpu.make_async_copy(
            amp.at[pl.ds(part * PART + chunk(j), CHUNK)], held[parity][part], row_sem.at[parity, part]
        )

    load(0, 0, 0).start()
    load(0, 0, 1).start()
    load_b.start()
    load(1, 1, 0).start()
    load(1, 1, 1).start()

    barrier = pltpu.get_barrier_semaphore()

    def greet(w, group):
        pl.semaphore_signal(barrier, inc=1, device_id=(w, group), device_id_type=MESH)

    greet(flip, g)
    greet(v, h)
    greet(flip, h)

    @pl.loop(1, N_VV // 2)
    def _(k):
        p = lax.rem(v // 4 * 2 + c + k, N_VV // 2)
        greet(p // 2 * 4 + xh * 2 + lax.rem(p, 2), g)

    pl.semaphore_wait(barrier, N_VV // 2 + 2)

    mine = place(labels, panel[0], pair[0])
    theirs = place(labels, panel[0], other_pair[0])

    def gives(j):
        row = chunk(j)
        here = a.at[pl.ds(g * HALF + row, CHUNK)]
        first = pltpu.make_async_remote_copy(
            src_ref=here,
            dst_ref=here,
            send_sem=give_sem,
            recv_sem=get_sem.at[row // CHUNK],
            device_id=(v, h),
            device_id_type=MESH,
        )
        second = pltpu.make_async_remote_copy(
            src_ref=other.at[pl.ds(row, CHUNK)],
            dst_ref=a.at[pl.ds(g * HALF + PART + row, CHUNK)],
            send_sem=give_sem,
            recv_sem=get_sem.at[PART // CHUNK + row // CHUNK],
            device_id=(flip, h),
            device_id_type=MESH,
        )
        return first, second

    def multiply(q0, q1):
        @pl.loop(0, ROWS // COLS)
        def _(n):
            col = pl.multiple_of(n * COLS, COLS)
            rows = jnp.concatenate([a[pl.ds(pl.multiple_of(q * CHUNK, CHUNK), CHUNK), :] for q in (q0, q1)], axis=0)
            part = lax.dot_general(
                rows, b[pl.ds(col, COLS), :], (((1,), (1,)), ((), ())), preferred_element_type=jnp.float32
            )
            part = part.astype(jnp.bfloat16).reshape(8, OWN, COLS)
            prod[pl.ds(q0 * 4, 4), :, pl.ds(col, COLS)] = part[:4]
            prod[pl.ds(q1 * 4, 4), :, pl.ds(col, COLS)] = part[4:]

    def push(source, w, sender):
        @pl.when(w == v)
        def _():
            pltpu.make_async_copy(source, recv.at[sender], self_sem).start()

        @pl.when(w != v)
        def _():
            pltpu.make_async_remote_copy(
                src_ref=source,
                dst_ref=recv.at[sender],
                send_sem=send_sem,
                recv_sem=recv_sem,
                device_id=(w, g),
                device_id_type=MESH,
            ).start()

    def near(q):
        @pl.loop(0, 2)
        def _(t):
            w = q * 4 + xh * 2 + lax.rem(c + t + 1, 2)
            push(prod.at[w], w, v)

    def crossing(k):
        i = k // 2
        half = lax.rem(z // 2 + k + 1, 2)
        n = lax.rem(i, 4)
        dy = lax.rem(n + 1, 4)
        return (2 * half + lax.rem(z + 1 + i // 4, 2)) * 4 + lax.rem(y + turn * dy + 4, 4)

    def across(u):
        q, core = crossing(u // 2), lax.rem(c + u + 1, 2)
        return pltpu.make_async_remote_copy(
            src_ref=prod.at[q * 4 + 2 - xh * 2 + core],
            dst_ref=stage.at[q * 2 + core],
            send_sem=x_send.at[u],
            recv_sem=x_recv.at[u],
            device_id=(flip, g),
            device_id_type=MESH,
        )

    def forward(u):
        across(u).wait_recv()
        q, core = crossing(u // 2), lax.rem(c + u + 1, 2)
        push(stage.at[q * 2 + core], q * 4 + xh * 2 + core, flip)

    @pl.loop(0, 2)
    def _(i):
        for parity in range(2):
            j = 2 * i + parity
            row = chunk(j)
            first, second = gives(j)
            load(j, parity, 0).wait()
            choose(held[parity][0], mine, a, pl.multiple_of(g * HALF + row, CHUNK))
            first.start()

            @pl.when(i == 0)
            def _():
                load(j + 2, parity, 0).start()

            load(j, parity, 1).wait()
            choose(held[parity][1], theirs, other, row)
            second.start()
            choose(held[parity][1], mine, a, pl.multiple_of(g * HALF + PART + row, CHUNK))

            @pl.when(i == 0)
            def _():
                load(j + 2, parity, 1).start()

            if parity == 0:

                @pl.when(i == 0)
                def _():
                    load_b.wait()

            mine_at = 8 * g + row // CHUNK
            multiply(mine_at, mine_at + 4)
            near(mine_at + 4 * lax.rem(z, 2))
            near(mine_at + 4 * lax.rem(z + 1, 2))

    @pl.loop(0, 4)
    def _(i):
        y4 = lax.rem(y + turn * i + 4, 4)
        for s in range(2):
            q = 8 * h + 4 * s + y4
            here = a.at[pl.ds(q * CHUNK, CHUNK)]
            pltpu.make_async_remote_copy(
                here, here, give_sem, get_sem.at[4 * s + y4], device_id=(v, h), device_id_type=MESH
            ).wait_recv()
        multiply(8 * h + y4, 8 * h + 4 + y4)
        near(8 * h + 4 * lax.rem(z, 2) + y4)
        near(8 * h + 4 * lax.rem(z + 1, 2) + y4)

        @pl.when(i == 3)
        def _():
            for u in range(WINDOW):
                across(u).start()

    @pl.loop(0, CROSS)
    def _(u):
        forward(u)

        @pl.when(u + WINDOW < CROSS)
        def _():
            across(u + WINDOW).start()

    for j in range(PART // CHUNK):
        for copy in gives(j):
            copy.wait_send()

    @pl.loop(0, CROSS)
    def _(u):
        across(u).wait_send()

    pltpu.make_async_copy(prod.at[pl.ds(0, 2)], recv.at[pl.ds(0, 2)], self_sem).wait()
    rest = pltpu.make_async_remote_copy(
        src_ref=prod.at[pl.ds(0, N_VV - 2)],
        dst_ref=recv.at[pl.ds(0, N_VV - 2)],
        send_sem=send_sem,
        recv_sem=recv_sem,
        device_id=(flip, g),
        device_id_type=MESH,
    )
    rest.wait_send()
    rest.wait_recv()


def ladder(labels, pair, other_pair, panel, amp, integrals):
    hbm = pl.BlockSpec(memory_space=pl.ANY)
    smem = pl.BlockSpec(memory_space=pltpu.SMEM)
    return pl.pallas_call(
        ladder_kernel,
        name="ladder",
        out_shape=pltpu.VMEM((N_VV, OWN, ROWS), jnp.bfloat16),
        in_specs=[smem] * 4 + [hbm] * 2,
        out_specs=pl.BlockSpec(memory_space=pltpu.VMEM),
        scratch_shapes=[
            pltpu.VMEM((IJ, KP), jnp.bfloat16),
            pltpu.VMEM((ROWS, KP), jnp.bfloat16),
            pltpu.VMEM((N_VV, OWN, ROWS), jnp.bfloat16),
            pltpu.VMEM((N_VV // 2, OWN, ROWS), jnp.bfloat16),
            pltpu.VMEM((PART, KP), jnp.bfloat16),
            pltpu.VMEM((CHUNK, DW * NV), jnp.bfloat16),
            pltpu.VMEM((CHUNK, DW * NV), jnp.bfloat16),
            pltpu.VMEM((CHUNK, DW * NV), jnp.bfloat16),
            pltpu.VMEM((CHUNK, DW * NV), jnp.bfloat16),
            pltpu.SemaphoreType.DMA,
            pltpu.SemaphoreType.DMA((2, 2)),
            pltpu.SemaphoreType.DMA,
            pltpu.SemaphoreType.DMA((HALF // CHUNK,)),
            pltpu.SemaphoreType.DMA,
            pltpu.SemaphoreType.DMA,
            pltpu.SemaphoreType.DMA,
            pltpu.SemaphoreType.DMA((CROSS,)),
            pltpu.SemaphoreType.DMA((CROSS,)),
        ],
        compiler_params=pltpu.CompilerParams(
            collective_id=0, has_side_effects=True, vmem_limit_bytes=48 * MIB
        ),
        cost_estimate=pl.CostEstimate(flops=2 * IJ * ROWS * KP, bytes_accessed=60 * MIB, transcendentals=0),
    )(labels, pair, other_pair, panel, amp, integrals)


TCOL = 768


def swap_kernel(x, out, buf, sem):
    row = lax.broadcasted_iota(jnp.int32, (256, 256), 0)
    col = lax.broadcasted_iota(jnp.int32, (256, 256), 1)
    perm = jnp.where(lax.rem(row, 16) * 16 + row // 16 == col, 1.0, 0.0).astype(jnp.bfloat16)

    def result(i, n):
        part = (pl.ds(i * 16, 16), slice(None), pl.ds(n * TCOL, TCOL))
        return pltpu.make_async_copy(buf.at[part], out.at[part], sem.at[i, n])

    for i in range(OWN // 16):
        for n in range(ROWS // TCOL):
            for s in range(N_VV // 16):
                block = x[pl.ds(s * 16, 16), pl.ds(i * 16, 16), pl.ds(n * TCOL, TCOL)].reshape(256, TCOL)
                part = jnp.dot(perm, block, preferred_element_type=jnp.float32)
                buf[pl.ds(i * 16, 16), pl.ds(s * 16, 16), pl.ds(n * TCOL, TCOL)] = part.astype(jnp.bfloat16).reshape(16, 16, TCOL)
            result(i, n).start()
    for i in range(OWN // 16):
        for n in range(ROWS // TCOL):
            result(i, n).wait()


def swap(x):
    return pl.pallas_call(
        swap_kernel,
        name="swap",
        out_shape=jax.ShapeDtypeStruct((OWN, N_VV, ROWS), jnp.bfloat16),
        in_specs=[pl.BlockSpec(memory_space=pltpu.VMEM)],
        out_specs=pl.BlockSpec(memory_space=pl.ANY),
        scratch_shapes=[
            pltpu.VMEM((OWN, N_VV, ROWS), jnp.bfloat16),
            pltpu.SemaphoreType.DMA((OWN // 16, ROWS // TCOL)),
        ],
        compiler_params=pltpu.CompilerParams(vmem_limit_bytes=24 * MIB),
        cost_estimate=pl.CostEstimate(flops=0, bytes_accessed=2 * IJ * ROWS * 2, transcendentals=0),
    )(x)


def shards(integrals, amplitudes, orbital_irrep, pair_irrep, panel_block):
    flipped = [(i, i ^ 2) for i in range(N_VV)]
    other_irrep = lax.ppermute(pair_irrep, "vv", flipped)
    return swap(ladder(orbital_irrep, pair_irrep, other_irrep, panel_block, amplitudes, integrals))


def solution(mesh):
    return jax.shard_map(
        shards,
        mesh=mesh,
        in_specs=(P("vv", "grp", None), P("grp", None), P(), P("vv"), P()),
        out_specs=P("vv", None, "grp"),
        check_vma=False,
    )
```

```python
import functools

import jax
import jax.numpy as jnp
from jax import lax
from jax.experimental import pallas as pl
from jax.experimental.pallas import tpu as pltpu
from jax.sharding import PartitionSpec as P

NIRR = 8
BS = 96
DW = 16
NV = NIRR * BS
KP = DW * BS
ROWS = 2304
IJ = 2048
HALF = IJ // 2
N_VV = 64
OWN = IJ // N_VV
CHUNK = 128
WINDOW = 4
CROSS = N_VV // 2
COLS = 768
MESH = pl.DeviceIdType.MESH
PART = HALF // 2
MIB = 1024 * 1024


def place(labels, panel, irrep):
    panel_irrep = jnp.int32(0)
    for k in range(NIRR):
        panel_irrep += jnp.where(panel == k, labels[k * BS], jnp.int32(0))
    target = irrep ^ panel_irrep
    allowed = jnp.int32(0)
    for k in range(NIRR):
        allowed += jnp.where(labels[k * BS] == target, jnp.int32(k), jnp.int32(0))
    return allowed


def choose(rows, allowed, out, row):
    lane = lax.broadcasted_iota(jnp.int32, (CHUNK, 128), 1)
    upper, rest = allowed // 4, lax.rem(allowed, 4)
    off = lax.rem(allowed * BS, 128)
    for q in range(DW // 4):
        w = []
        for j in range(4):
            start = (q * 4 + j) * NV
            t = [
                jnp.where(upper == 1, rows[:, start + 384 + n : start + 512 + n], rows[:, start + n : start + 128 + n]).astype(jnp.float32)
                for n in (0, 128, 256)
            ]
            low = jnp.where(rest < 2, t[0], jnp.where(rest == 2, t[1], t[2]))
            x = jnp.concatenate([low, jnp.where(rest < 2, t[1], t[2])], axis=1)
            shift = (96 * j) % 128
            w.append(pltpu.roll(x, lax.rem(shift - off + 256, 256), 1))
        t0 = jnp.where(lane < 96, w[0][:, :128], w[1][:, :128])
        t1 = jnp.where(lane < 64, w[1][:, 128:], w[2][:, :128])
        t2 = jnp.where(lane < 32, w[2][:, 128:], w[3][:, :128])
        out[pl.ds(row, CHUNK), q * 384 : (q + 1) * 384] = jnp.concatenate([t0, t1, t2], axis=1).astype(jnp.bfloat16)


def ladder_kernel(labels, pair, panel, amp, integrals, recv, a, b, prod, stage, other, a0, a1, b0, b1, tag_out, tag_in, tag_sem, load_sem, row_sem, give_sem, get_sem, send_sem, recv_sem, self_sem, x_send, x_recv):
    v = lax.axis_index("vv")
    g = lax.axis_index("grp")
    h = 1 - g
    z, y = v // 16, lax.rem(v // 4, 4)
    xh, c = lax.rem(v // 2, 2), lax.rem(v, 2)
    flip = v + 2 - 4 * xh
    turn = 1 - 2 * c
    load_b = pltpu.make_async_copy(integrals.at[0], b, load_sem)
    held = ((a0, b0), (a1, b1))

    def chunk(j):
        return pl.multiple_of(lax.rem(y + turn * j + 4, 4) * CHUNK, CHUNK)

    def load(j, parity, part):
        return pltpu.make_async_copy(
            amp.at[pl.ds(part * PART + chunk(j), CHUNK)], held[parity][part], row_sem.at[parity, part]
        )

    load(0, 0, 0).start()
    load(0, 0, 1).start()
    load_b.start()
    load(1, 1, 0).start()
    load(1, 1, 1).start()

    tag_out[...] = jnp.full((8, 128), pair[0], jnp.int32)
    barrier = pltpu.get_barrier_semaphore()

    def greet(w, group):
        pl.semaphore_signal(barrier, inc=1, device_id=(w, group), device_id_type=MESH)

    greet(flip, g)
    greet(v, h)
    greet(flip, h)

    @pl.loop(1, N_VV // 2)
    def _(k):
        p = lax.rem(v // 4 * 2 + c + k, N_VV // 2)
        greet(p // 2 * 4 + xh * 2 + lax.rem(p, 2), g)

    pl.semaphore_wait(barrier, N_VV // 2 + 2)

    tag = pltpu.make_async_remote_copy(
        src_ref=tag_out,
        dst_ref=tag_in,
        send_sem=tag_sem.at[0],
        recv_sem=tag_sem.at[1],
        device_id=(flip, g),
        device_id_type=MESH,
    )
    tag.start()
    mine = place(labels, panel[0], pair[0])

    def gives(j):
        row = chunk(j)
        here = a.at[pl.ds(g * HALF + row, CHUNK)]
        first = pltpu.make_async_remote_copy(
            src_ref=here,
            dst_ref=here,
            send_sem=give_sem,
            recv_sem=get_sem.at[row // CHUNK],
            device_id=(v, h),
            device_id_type=MESH,
        )
        second = pltpu.make_async_remote_copy(
            src_ref=other.at[pl.ds(row, CHUNK)],
            dst_ref=a.at[pl.ds(g * HALF + PART + row, CHUNK)],
            send_sem=give_sem,
            recv_sem=get_sem.at[PART // CHUNK + row // CHUNK],
            device_id=(flip, h),
            device_id_type=MESH,
        )
        return first, second

    def multiply(q0, q1):
        @pl.loop(0, ROWS // COLS)
        def _(n):
            col = pl.multiple_of(n * COLS, COLS)
            rows = jnp.concatenate([a[pl.ds(pl.multiple_of(q * CHUNK, CHUNK), CHUNK), :] for q in (q0, q1)], axis=0)
            part = lax.dot_general(
                rows, b[pl.ds(col, COLS), :], (((1,), (1,)), ((), ())), preferred_element_type=jnp.float32
            )
            part = part.astype(jnp.bfloat16).reshape(8, OWN, COLS)
            prod[pl.ds(q0 * 4, 4), :, pl.ds(col, COLS)] = part[:4]
            prod[pl.ds(q1 * 4, 4), :, pl.ds(col, COLS)] = part[4:]

    def push(source, w, sender):
        @pl.when(w == v)
        def _():
            pltpu.make_async_copy(source, recv.at[sender], self_sem).start()

        @pl.when(w != v)
        def _():
            pltpu.make_async_remote_copy(
                src_ref=source,
                dst_ref=recv.at[sender],
                send_sem=send_sem,
                recv_sem=recv_sem,
                device_id=(w, g),
                device_id_type=MESH,
            ).start()

    def near(q):
        @pl.loop(0, 2)
        def _(t):
            w = q * 4 + xh * 2 + lax.rem(c + t + 1, 2)
            push(prod.at[w], w, v)

    def crossing(k):
        i = k // 2
        half = lax.rem(z // 2 + k + 1, 2)
        n = lax.rem(i, 4)
        dy = lax.rem(n + 1, 4)
        return (2 * half + lax.rem(z + k + i // 4, 2)) * 4 + lax.rem(y + turn * dy + 4, 4)

    def across(u):
        q, core = crossing(u // 2), lax.rem(c + u + 1, 2)
        return pltpu.make_async_remote_copy(
            src_ref=prod.at[q * 4 + 2 - xh * 2 + core],
            dst_ref=stage.at[q * 2 + core],
            send_sem=x_send.at[u],
            recv_sem=x_recv.at[u],
            device_id=(flip, g),
            device_id_type=MESH,
        )

    def forward(u):
        q, core = crossing(u // 2), lax.rem(c + u + 1, 2)
        push(stage.at[q * 2 + core], q * 4 + xh * 2 + core, flip)

    def first_part(j, parity):
        load(j, parity, 0).wait()
        choose(held[parity][0], mine, a, pl.multiple_of(g * HALF + chunk(j), CHUNK))
        gives(j)[0].start()

    first_part(0, 0)
    load(2, 0, 0).start()
    tag.wait()
    theirs = place(labels, panel[0], jnp.max(tag_in[...]))

    @pl.loop(0, 2)
    def _(i):
        for parity in range(2):
            j = 2 * i + parity
            row = chunk(j)
            if parity == 0:

                @pl.when(i == 1)
                def _():
                    first_part(2, 0)
            else:
                first_part(j, 1)

                @pl.when(i == 0)
                def _():
                    load(3, 1, 0).start()

            load(j, parity, 1).wait()
            choose(held[parity][1], theirs, other, row)
            gives(j)[1].start()
            choose(held[parity][1], mine, a, pl.multiple_of(g * HALF + PART + row, CHUNK))

            @pl.when(i == 0)
            def _():
                load(j + 2, parity, 1).start()

            if parity == 0:

                @pl.when(i == 0)
                def _():
                    load_b.wait()

            mine_at = 8 * g + row // CHUNK
            multiply(mine_at, mine_at + 4)
            near(mine_at + 4 * lax.rem(z, 2))
            near(mine_at + 4 * lax.rem(z + 1, 2))

    @pl.loop(0, 4)
    def _(i):
        y4 = lax.rem(y + turn * i + 4, 4)
        for s in range(2):
            q = 8 * h + 4 * s + y4
            here = a.at[pl.ds(q * CHUNK, CHUNK)]
            pltpu.make_async_remote_copy(
                here, here, give_sem, get_sem.at[4 * s + y4], device_id=(v, h), device_id_type=MESH
            ).wait_recv()
        multiply(8 * h + y4, 8 * h + 4 + y4)
        near(8 * h + 4 * lax.rem(z, 2) + y4)
        near(8 * h + 4 * lax.rem(z + 1, 2) + y4)

        @pl.when(i == 3)
        def _():
            for u in range(WINDOW):
                across(u).start()

    @pl.loop(0, CROSS)
    def _(u):
        across(u).wait_recv()

        @pl.when(u + WINDOW < CROSS)
        def _():
            across(u + WINDOW).start()

        forward(u)

    for j in range(PART // CHUNK):
        for copy in gives(j):
            copy.wait_send()

    @pl.loop(0, CROSS)
    def _(u):
        across(u).wait_send()

    pltpu.make_async_copy(prod.at[pl.ds(0, 2)], recv.at[pl.ds(0, 2)], self_sem).wait()
    rest = pltpu.make_async_remote_copy(
        src_ref=prod.at[pl.ds(0, N_VV - 2)],
        dst_ref=recv.at[pl.ds(0, N_VV - 2)],
        send_sem=send_sem,
        recv_sem=recv_sem,
        device_id=(flip, g),
        device_id_type=MESH,
    )
    rest.wait_send()
    rest.wait_recv()


def ladder(labels, pair, panel, amp, integrals):
    hbm = pl.BlockSpec(memory_space=pl.ANY)
    smem = pl.BlockSpec(memory_space=pltpu.SMEM)
    return pl.pallas_call(
        ladder_kernel,
        name="ladder",
        out_shape=pltpu.VMEM((N_VV, OWN, ROWS), jnp.bfloat16),
        in_specs=[smem] * 3 + [hbm] * 2,
        out_specs=pl.BlockSpec(memory_space=pltpu.VMEM),
        scratch_shapes=[
            pltpu.VMEM((IJ, KP), jnp.bfloat16),
            pltpu.VMEM((ROWS, KP), jnp.bfloat16),
            pltpu.VMEM((N_VV, OWN, ROWS), jnp.bfloat16),
            pltpu.VMEM((N_VV // 2, OWN, ROWS), jnp.bfloat16),
            pltpu.VMEM((PART, KP), jnp.bfloat16),
            pltpu.VMEM((CHUNK, DW * NV), jnp.bfloat16),
            pltpu.VMEM((CHUNK, DW * NV), jnp.bfloat16),
            pltpu.VMEM((CHUNK, DW * NV), jnp.bfloat16),
            pltpu.VMEM((CHUNK, DW * NV), jnp.bfloat16),
            pltpu.VMEM((8, 128), jnp.int32),
            pltpu.VMEM((8, 128), jnp.int32),
            pltpu.SemaphoreType.DMA((2,)),
            pltpu.SemaphoreType.DMA,
            pltpu.SemaphoreType.DMA((2, 2)),
            pltpu.SemaphoreType.DMA,
            pltpu.SemaphoreType.DMA((HALF // CHUNK,)),
            pltpu.SemaphoreType.DMA,
            pltpu.SemaphoreType.DMA,
            pltpu.SemaphoreType.DMA,
            pltpu.SemaphoreType.DMA((CROSS,)),
            pltpu.SemaphoreType.DMA((CROSS,)),
        ],
        compiler_params=pltpu.CompilerParams(
            collective_id=0, has_side_effects=True, vmem_limit_bytes=48 * MIB
        ),
        cost_estimate=pl.CostEstimate(flops=2 * IJ * ROWS * KP, bytes_accessed=60 * MIB, transcendentals=0),
    )(labels, pair, panel, amp, integrals)


TCOL = 768


def swap_kernel(x, out, buf, sem):
    row = lax.broadcasted_iota(jnp.int32, (256, 256), 0)
    col = lax.broadcasted_iota(jnp.int32, (256, 256), 1)
    perm = jnp.where(lax.rem(row, 16) * 16 + row // 16 == col, 1.0, 0.0).astype(jnp.bfloat16)

    def result(i, n):
        part = (pl.ds(i * 16, 16), slice(None), pl.ds(n * TCOL, TCOL))
        return pltpu.make_async_copy(buf.at[part], out.at[part], sem.at[i, n])

    for i in range(OWN // 16):
        for n in range(ROWS // TCOL):
            for s in range(N_VV // 16):
                block = x[pl.ds(s * 16, 16), pl.ds(i * 16, 16), pl.ds(n * TCOL, TCOL)].reshape(256, TCOL)
                part = jnp.dot(perm, block, preferred_element_type=jnp.float32)
                buf[pl.ds(i * 16, 16), pl.ds(s * 16, 16), pl.ds(n * TCOL, TCOL)] = part.astype(jnp.bfloat16).reshape(16, 16, TCOL)
            result(i, n).start()
    for i in range(OWN // 16):
        for n in range(ROWS // TCOL):
            result(i, n).wait()


def swap(x):
    return pl.pallas_call(
        swap_kernel,
        name="swap",
        out_shape=jax.ShapeDtypeStruct((OWN, N_VV, ROWS), jnp.bfloat16),
        in_specs=[pl.BlockSpec(memory_space=pltpu.VMEM)],
        out_specs=pl.BlockSpec(memory_space=pl.ANY),
        scratch_shapes=[
            pltpu.VMEM((OWN, N_VV, ROWS), jnp.bfloat16),
            pltpu.SemaphoreType.DMA((OWN // 16, ROWS // TCOL)),
        ],
        compiler_params=pltpu.CompilerParams(vmem_limit_bytes=24 * MIB),
        cost_estimate=pl.CostEstimate(flops=0, bytes_accessed=2 * IJ * ROWS * 2, transcendentals=0),
    )(x)


def shards(integrals, amplitudes, orbital_irrep, pair_irrep, panel_block):
    return swap(ladder(orbital_irrep, pair_irrep, panel_block, amplitudes, integrals))


def solution(mesh):
    return jax.shard_map(
        shards,
        mesh=mesh,
        in_specs=(P("vv", "grp", None), P("grp", None), P(), P("vv"), P()),
        out_specs=P("vv", None, "grp"),
        check_vma=False,
    )
```

```python
import functools

import jax
import jax.numpy as jnp
from jax import lax
from jax.experimental import pallas as pl
from jax.experimental.pallas import tpu as pltpu
from jax.sharding import PartitionSpec as P

NIRR = 8
BS = 96
DW = 16
NV = NIRR * BS
KP = DW * BS
ROWS = 2304
IJ = 2048
HALF = IJ // 2
N_VV = 64
OWN = IJ // N_VV
CHUNK = 128
WINDOW = 4
CROSS = N_VV // 2
COLS = 768
MESH = pl.DeviceIdType.MESH
PART = HALF // 2
MIB = 1024 * 1024


def place(labels, panel, irrep):
    panel_irrep = jnp.int32(0)
    for k in range(NIRR):
        panel_irrep += jnp.where(panel == k, labels[k * BS], jnp.int32(0))
    target = irrep ^ panel_irrep
    allowed = jnp.int32(0)
    for k in range(NIRR):
        allowed += jnp.where(labels[k * BS] == target, jnp.int32(k), jnp.int32(0))
    return allowed


def choose(rows, allowed, out, row):
    lane = lax.broadcasted_iota(jnp.int32, (CHUNK, 128), 1)
    upper, rest = allowed // 4, lax.rem(allowed, 4)
    off = lax.rem(allowed * BS, 128)
    for q in range(DW // 4):
        w = []
        for j in range(4):
            start = (q * 4 + j) * NV
            t = [
                jnp.where(upper == 1, rows[:, start + 384 + n : start + 512 + n], rows[:, start + n : start + 128 + n]).astype(jnp.float32)
                for n in (0, 128, 256)
            ]
            low = jnp.where(rest < 2, t[0], jnp.where(rest == 2, t[1], t[2]))
            x = jnp.concatenate([low, jnp.where(rest < 2, t[1], t[2])], axis=1)
            shift = (96 * j) % 128
            w.append(pltpu.roll(x, lax.rem(shift - off + 256, 256), 1))
        t0 = jnp.where(lane < 96, w[0][:, :128], w[1][:, :128])
        t1 = jnp.where(lane < 64, w[1][:, 128:], w[2][:, :128])
        t2 = jnp.where(lane < 32, w[2][:, 128:], w[3][:, :128])
        out[pl.ds(row, CHUNK), q * 384 : (q + 1) * 384] = jnp.concatenate([t0, t1, t2], axis=1).astype(jnp.bfloat16)


def ladder_kernel(labels, pair, panel, amp, integrals, recv, a, b, prod, stage, other, a0, a1, b0, b1, tag_out, tag_in, tag_sem, ready_sem, load_sem, row_sem, give_sem, get_sem, send_sem, recv_sem, self_sem, x_send, x_recv):
    v = lax.axis_index("vv")
    g = lax.axis_index("grp")
    h = 1 - g
    z, y = v // 16, lax.rem(v // 4, 4)
    xh, c = lax.rem(v // 2, 2), lax.rem(v, 2)
    flip = v + 2 - 4 * xh
    turn = 1 - 2 * c
    load_b = pltpu.make_async_copy(integrals.at[0], b, load_sem)
    held = ((a0, b0), (a1, b1))

    def chunk(j):
        return pl.multiple_of(lax.rem(y + turn * j + 4, 4) * CHUNK, CHUNK)

    def load(j, parity, part):
        return pltpu.make_async_copy(
            amp.at[pl.ds(part * PART + chunk(j), CHUNK)], held[parity][part], row_sem.at[parity, part]
        )

    load(0, 0, 0).start()
    load(0, 0, 1).start()
    load_b.start()
    load(1, 1, 0).start()
    load(1, 1, 1).start()

    tag_out[...] = jnp.full((8, 128), pair[0], jnp.int32)
    barrier = pltpu.get_barrier_semaphore()

    def greet(w, group):
        pl.semaphore_signal(barrier, inc=1, device_id=(w, group), device_id_type=MESH)

    greet(flip, g)
    greet(v, h)
    greet(flip, h)

    @pl.loop(1, N_VV // 2)
    def _(k):
        p = lax.rem(v // 4 * 2 + c + k, N_VV // 2)
        greet(p // 2 * 4 + xh * 2 + lax.rem(p, 2), g)

    pl.semaphore_wait(barrier, N_VV // 2 + 2)

    tag = pltpu.make_async_remote_copy(
        src_ref=tag_out,
        dst_ref=tag_in,
        send_sem=tag_sem.at[0],
        recv_sem=tag_sem.at[1],
        device_id=(flip, g),
        device_id_type=MESH,
    )
    tag.start()
    mine = place(labels, panel[0], pair[0])

    def gives(j):
        row = chunk(j)
        here = a.at[pl.ds(g * HALF + row, CHUNK)]
        first = pltpu.make_async_remote_copy(
            src_ref=here,
            dst_ref=here,
            send_sem=give_sem,
            recv_sem=get_sem.at[row // CHUNK],
            device_id=(v, h),
            device_id_type=MESH,
        )
        second = pltpu.make_async_remote_copy(
            src_ref=other.at[pl.ds(row, CHUNK)],
            dst_ref=a.at[pl.ds(g * HALF + PART + row, CHUNK)],
            send_sem=give_sem,
            recv_sem=get_sem.at[PART // CHUNK + row // CHUNK],
            device_id=(flip, h),
            device_id_type=MESH,
        )
        return first, second

    def multiply(q0, q1):
        @pl.loop(0, ROWS // COLS)
        def _(n):
            col = pl.multiple_of(n * COLS, COLS)
            rows = jnp.concatenate([a[pl.ds(pl.multiple_of(q * CHUNK, CHUNK), CHUNK), :] for q in (q0, q1)], axis=0)
            part = lax.dot_general(
                rows, b[pl.ds(col, COLS), :], (((1,), (1,)), ((), ())), preferred_element_type=jnp.float32
            )
            part = part.astype(jnp.bfloat16).reshape(8, OWN, COLS)
            prod[pl.ds(q0 * 4, 4), :, pl.ds(col, COLS)] = part[:4]
            prod[pl.ds(q1 * 4, 4), :, pl.ds(col, COLS)] = part[4:]

    def push(source, w, sender):
        @pl.when(w == v)
        def _():
            pltpu.make_async_copy(source, recv.at[sender], self_sem).start()

        @pl.when(w != v)
        def _():
            pltpu.make_async_remote_copy(
                src_ref=source,
                dst_ref=recv.at[sender],
                send_sem=send_sem,
                recv_sem=recv_sem,
                device_id=(w, g),
                device_id_type=MESH,
            ).start()

    def near(q):
        @pl.loop(0, 2)
        def _(t):
            w = q * 4 + xh * 2 + lax.rem(c + t + 1, 2)
            push(prod.at[w], w, v)

    def crossing(k):
        i = k // 2
        half = lax.rem(z // 2 + k + 1, 2)
        n = lax.rem(i, 4)
        dy = lax.rem(n + 1, 4)
        return (2 * half + lax.rem(z + k + i // 4, 2)) * 4 + lax.rem(y + turn * dy + 4, 4)

    def across(u):
        q, core = crossing(u // 2), lax.rem(c + u + 1, 2)
        return pltpu.make_async_remote_copy(
            src_ref=prod.at[q * 4 + 2 - xh * 2 + core],
            dst_ref=stage.at[q * 2 + core],
            send_sem=x_send.at[u],
            recv_sem=x_recv.at[u],
            device_id=(flip, g),
            device_id_type=MESH,
        )

    def forward(u):
        q, core = crossing(u // 2), lax.rem(c + u + 1, 2)
        push(stage.at[q * 2 + core], q * 4 + xh * 2 + core, flip)

    def first_part(j, parity):
        load(j, parity, 0).wait()
        choose(held[parity][0], mine, a, pl.multiple_of(g * HALF + chunk(j), CHUNK))
        gives(j)[0].start()

    first_part(0, 0)
    load(2, 0, 0).start()
    tag.wait()
    theirs = place(labels, panel[0], jnp.max(tag_in[...]))

    @pl.loop(0, 2)
    def _(i):
        for parity in range(2):
            j = 2 * i + parity
            row = chunk(j)
            if parity == 0:

                @pl.when(i == 1)
                def _():
                    first_part(2, 0)
            else:
                first_part(j, 1)

                @pl.when(i == 0)
                def _():
                    load(3, 1, 0).start()

            load(j, parity, 1).wait()
            choose(held[parity][1], theirs, other, row)
            gives(j)[1].start()
            choose(held[parity][1], mine, a, pl.multiple_of(g * HALF + PART + row, CHUNK))

            @pl.when(i == 0)
            def _():
                load(j + 2, parity, 1).start()

            if parity == 0:

                @pl.when(i == 0)
                def _():
                    load_b.wait()

            mine_at = 8 * g + row // CHUNK
            multiply(mine_at, mine_at + 4)
            near(mine_at + 4 * lax.rem(z, 2))
            near(mine_at + 4 * lax.rem(z + 1, 2))

    @pl.loop(0, 4)
    def _(i):
        y4 = lax.rem(y + turn * i + 4, 4)
        for s in range(2):
            q = 8 * h + 4 * s + y4
            here = a.at[pl.ds(q * CHUNK, CHUNK)]
            pltpu.make_async_remote_copy(
                here, here, give_sem, get_sem.at[4 * s + y4], device_id=(v, h), device_id_type=MESH
            ).wait_recv()

        @pl.when(i == 3)
        def _():
            for w, group in ((v, h), (flip, h), (flip, g)):
                pl.semaphore_signal(ready_sem, inc=1, device_id=(w, group), device_id_type=MESH)

        @pl.when(i == 3)
        def _():
            pl.semaphore_wait(ready_sem, 3)
            for u in range(WINDOW):
                across(u).start()

        multiply(8 * h + y4, 8 * h + 4 + y4)
        near(8 * h + 4 * lax.rem(z, 2) + y4)
        near(8 * h + 4 * lax.rem(z + 1, 2) + y4)

    @pl.loop(0, CROSS)
    def _(u):
        across(u).wait_recv()

        @pl.when(u + WINDOW < CROSS)
        def _():
            across(u + WINDOW).start()

        forward(u)

    for j in range(PART // CHUNK):
        for copy in gives(j):
            copy.wait_send()

    @pl.loop(0, CROSS)
    def _(u):
        across(u).wait_send()

    pltpu.make_async_copy(prod.at[pl.ds(0, 2)], recv.at[pl.ds(0, 2)], self_sem).wait()
    rest = pltpu.make_async_remote_copy(
        src_ref=prod.at[pl.ds(0, N_VV - 2)],
        dst_ref=recv.at[pl.ds(0, N_VV - 2)],
        send_sem=send_sem,
        recv_sem=recv_sem,
        device_id=(flip, g),
        device_id_type=MESH,
    )
    rest.wait_send()
    rest.wait_recv()


def ladder(labels, pair, panel, amp, integrals):
    hbm = pl.BlockSpec(memory_space=pl.ANY)
    smem = pl.BlockSpec(memory_space=pltpu.SMEM)
    return pl.pallas_call(
        ladder_kernel,
        name="ladder",
        out_shape=pltpu.VMEM((N_VV, OWN, ROWS), jnp.bfloat16),
        in_specs=[smem] * 3 + [hbm] * 2,
        out_specs=pl.BlockSpec(memory_space=pltpu.VMEM),
        scratch_shapes=[
            pltpu.VMEM((IJ, KP), jnp.bfloat16),
            pltpu.VMEM((ROWS, KP), jnp.bfloat16),
            pltpu.VMEM((N_VV, OWN, ROWS), jnp.bfloat16),
            pltpu.VMEM((N_VV // 2, OWN, ROWS), jnp.bfloat16),
            pltpu.VMEM((PART, KP), jnp.bfloat16),
            pltpu.VMEM((CHUNK, DW * NV), jnp.bfloat16),
            pltpu.VMEM((CHUNK, DW * NV), jnp.bfloat16),
            pltpu.VMEM((CHUNK, DW * NV), jnp.bfloat16),
            pltpu.VMEM((CHUNK, DW * NV), jnp.bfloat16),
            pltpu.VMEM((8, 128), jnp.int32),
            pltpu.VMEM((8, 128), jnp.int32),
            pltpu.SemaphoreType.DMA((2,)),
            pltpu.SemaphoreType.REGULAR,
            pltpu.SemaphoreType.DMA,
            pltpu.SemaphoreType.DMA((2, 2)),
            pltpu.SemaphoreType.DMA,
            pltpu.SemaphoreType.DMA((HALF // CHUNK,)),
            pltpu.SemaphoreType.DMA,
            pltpu.SemaphoreType.DMA,
            pltpu.SemaphoreType.DMA,
            pltpu.SemaphoreType.DMA((CROSS,)),
            pltpu.SemaphoreType.DMA((CROSS,)),
        ],
        compiler_params=pltpu.CompilerParams(
            collective_id=0, has_side_effects=True, vmem_limit_bytes=48 * MIB
        ),
        cost_estimate=pl.CostEstimate(flops=2 * IJ * ROWS * KP, bytes_accessed=60 * MIB, transcendentals=0),
    )(labels, pair, panel, amp, integrals)


TCOL = 768


def swap_kernel(x, out, buf, sem):
    row = lax.broadcasted_iota(jnp.int32, (256, 256), 0)
    col = lax.broadcasted_iota(jnp.int32, (256, 256), 1)
    perm = jnp.where(lax.rem(row, 16) * 16 + row // 16 == col, 1.0, 0.0).astype(jnp.bfloat16)

    def result(i, n):
        part = (pl.ds(i * 16, 16), slice(None), pl.ds(n * TCOL, TCOL))
        return pltpu.make_async_copy(buf.at[part], out.at[part], sem.at[i, n])

    for i in range(OWN // 16):
        for n in range(ROWS // TCOL):
            for s in range(N_VV // 16):
                block = x[pl.ds(s * 16, 16), pl.ds(i * 16, 16), pl.ds(n * TCOL, TCOL)].reshape(256, TCOL)
                part = jnp.dot(perm, block, preferred_element_type=jnp.float32)
                buf[pl.ds(i * 16, 16), pl.ds(s * 16, 16), pl.ds(n * TCOL, TCOL)] = part.astype(jnp.bfloat16).reshape(16, 16, TCOL)
            result(i, n).start()
    for i in range(OWN // 16):
        for n in range(ROWS // TCOL):
            result(i, n).wait()


def swap(x):
    return pl.pallas_call(
        swap_kernel,
        name="swap",
        out_shape=jax.ShapeDtypeStruct((OWN, N_VV, ROWS), jnp.bfloat16),
        in_specs=[pl.BlockSpec(memory_space=pltpu.VMEM)],
        out_specs=pl.BlockSpec(memory_space=pl.ANY),
        scratch_shapes=[
            pltpu.VMEM((OWN, N_VV, ROWS), jnp.bfloat16),
            pltpu.SemaphoreType.DMA((OWN // 16, ROWS // TCOL)),
        ],
        compiler_params=pltpu.CompilerParams(vmem_limit_bytes=24 * MIB),
        cost_estimate=pl.CostEstimate(flops=0, bytes_accessed=2 * IJ * ROWS * 2, transcendentals=0),
    )(x)


def shards(integrals, amplitudes, orbital_irrep, pair_irrep, panel_block):
    return swap(ladder(orbital_irrep, pair_irrep, panel_block, amplitudes, integrals))


def solution(mesh):
    return jax.shard_map(
        shards,
        mesh=mesh,
        in_specs=(P("vv", "grp", None), P("grp", None), P(), P("vv"), P()),
        out_specs=P("vv", None, "grp"),
        check_vma=False,
    )
```
